512 devices in a mesh: rows: 64 (over z, y), blk: 8 (over x, core).
Axes of the slice: x: 4, y: 8, z: 8, core: 2. Of those that a mesh axis runs over, the one named last changes fastest.
Arguments:
- atom_desc: bfloat16 [1000, 32768], P(None, 'rows'), may hold values from -6 to 6
- sparse_panel: bfloat16 [2048, 1000], P('blk'), may hold values from -0.1875 to 0.1875
- atom_cell: int32 [32768], P('rows'), may hold values from 0 to 31, as said below
- energy_target: bfloat16 [2048], P('rows'), may hold values from -6 to 6
- force_counts: int32 [2048], P('rows'), may hold values from 0 to 1024, as said below
- force_atom: int32 [65536], P('rows'), may hold values from 0 to 511
- force_grad: bfloat16 [1000, 65536], P(None, 'rows'), may hold values from -6 to 6
- force_target: bfloat16 [65536], P('rows'), may hold values from -6 to 6
Outputs:
- gram_matrix: float32 [2048, 2048], P('rows', 'blk')
- right_side: float32 [2048], P('blk')
The draws below stay inside these ranges and needn't reach their ends.
Inputs may be any that keep to these rules, and one draw needn't show every extreme that they name: `force_counts`: each group's cells together hold at most 1024 force rows; some group holds exactly 1024, all in one of its cells; all groups together hold exactly 512 rows per group on average. `atom_cell`: an index among the cells of the atom's own group. `force_atom`: an index among the atoms of the slot's own group.
All inputs are finite; a program needn't handle non-finite values.
Results may differ from the reference program's by a relative error of at most 0.003.
Values may be sent and summed in bfloat16 or wider, within the bound.
A program may use at most 64 MiB of HBM per device.

```python
import jax
import jax.numpy as jnp
from jax import lax

D = 1000
M = 2048
CELLS_DEV = 32
ATOMS_DEV = 512
FCAP = 1024
FMEAN = 512
CELLS = 2048
ATOMS = 32768
FROWS = 65536
ROWS_ALL = 34816
N_ROWS = 64


def draw_force_counts(key, part):
    key = jax.random.fold_in(key, 11)
    first_key, second_key, third_key = jax.random.split(key, 3)
    groups = CELLS // CELLS_DEV
    spread = FCAP - FMEAN
    shifts = jax.random.randint(first_key, (groups,), 0, spread + 1)
    chosen = jax.random.randint(second_key, (), 0, groups)
    places = jnp.arange(groups)
    shifts = jnp.where(places == chosen, spread, jnp.where(places == (chosen + 1) % groups, 0, shifts))
    loads = FMEAN + shifts - jnp.roll(shifts, -1)
    cuts = jax.random.randint(third_key, (groups, CELLS_DEV - 1), 0, loads[:, None] + 1)
    cuts = jnp.where((places == chosen)[:, None], 0, cuts)
    cuts = jnp.sort(cuts, axis=1)
    bounds = jnp.concatenate([jnp.zeros((groups, 1), jnp.int32), cuts.astype(jnp.int32), loads[:, None].astype(jnp.int32)], axis=1)
    return (bounds[:, 1:] - bounds[:, :-1]).reshape(CELLS).astype(jnp.int32)


def draw_atom_cell(key, part):
    key = jax.random.fold_in(key, 5)
    empty_key, flag_key, chosen_key, full_key, fewer_key = jax.random.split(key, 5)
    groups = ATOMS // ATOMS_DEV
    empty_cell = jax.random.randint(empty_key, (groups, 1), 0, CELLS_DEV)
    flags = jax.random.randint(flag_key, (groups, 1), 0, 4) == 0
    chosen = jax.random.randint(chosen_key, (), 0, groups)
    flags = jnp.logical_or(flags, (jnp.arange(groups) == chosen)[:, None])
    every_cell = jax.random.randint(full_key, (groups, ATOMS_DEV), 0, CELLS_DEV)
    fewer_cells = jax.random.randint(fewer_key, (groups, ATOMS_DEV), 0, CELLS_DEV - 1)
    skipping = fewer_cells + (fewer_cells >= empty_cell).astype(jnp.int32)
    cells = jnp.where(flags, skipping, every_cell)
    return cells.reshape(ATOMS).astype(jnp.int32)


def place_ends(values, key, smallest, top_value):
    dims = values.shape
    place = [jax.random.randint(jax.random.fold_in(key, axis), (), 0, dims[axis]) for axis in range(len(dims))]
    values = values.at[tuple(place)].set(smallest)
    longest = dims.index(max(dims))
    place[longest] = (place[longest] + 1) % dims[longest]
    return values.at[tuple(place)].set(top_value)


def level_of(stream_key, dims, cuts, least, largest):
    level = 1.0
    for axis_at, shards_of in cuts:
        heights = jax.random.uniform(jax.random.fold_in(jax.random.fold_in(stream_key, 6), axis_at), (shards_of,), jnp.float32, least / len(cuts), largest / len(cuts))
        level = level * jnp.repeat(jnp.exp(heights), dims[axis_at] // shards_of).reshape((-1,) + (1,) * (len(dims) - 1 - axis_at))
    return level


def gaussian(rng, dims, scale, reach, cuts=(), kind=jnp.bfloat16):
    array = scale * jax.random.normal(rng, dims, jnp.float32)
    if cuts:
        array = array * level_of(rng, dims, cuts, -0.22, 0.18)
    return jnp.clip(array, -reach, reach).astype(kind)


def setup_inputs(seed: int = 0) -> dict:
    keys = jax.random.split(jax.random.key(seed), 9)
    atom_desc = gaussian(keys[0], (D, ATOMS), 1.0, 6.0, ((1, 64),))
    sparse_panel = gaussian(keys[1], (M, D), D ** -0.5, 0.1875, ((0, 8),))
    atom_cell = draw_atom_cell(jax.random.fold_in(keys[8], 71), 0)
    energy_target = gaussian(keys[3], (CELLS,), 1.0, 6.0, ((0, 64),))
    force_counts = draw_force_counts(jax.random.fold_in(keys[8], 71), 0)
    force_atom = place_ends(jax.random.randint(keys[5], (FROWS,), 0, ATOMS_DEV), jax.random.fold_in(keys[5], 1), 0, ATOMS_DEV - 1).astype(jnp.int32)
    force_grad = gaussian(keys[6], (D, FROWS), 1.0, 6.0, ((1, 64),))
    force_target = gaussian(keys[7], (FROWS,), 1.0, 6.0, ((0, 64),))
    return dict(atom_desc=atom_desc, sparse_panel=sparse_panel, atom_cell=atom_cell, energy_target=energy_target, force_counts=force_counts, force_atom=force_atom, force_grad=force_grad, force_target=force_target)


def device_rows(sparse_panel, atom_desc, atom_cell, energy_target, force_counts, force_atom, force_grad, force_target):
    products = jnp.dot(sparse_panel, atom_desc, preferred_element_type=jnp.float32)
    powered = products ** 4
    member_table = (atom_cell[None, :] == jnp.arange(CELLS_DEV, dtype=jnp.int32)[:, None]).astype(jnp.float32)
    members = jnp.maximum(jnp.sum(member_table, axis=1), 1.0)
    energy = jnp.dot(powered, member_table.T, precision=lax.Precision.HIGHEST) / members[None, :]
    live_rows = jnp.sum(force_counts)
    keep_mask = jnp.arange(FCAP, dtype=jnp.int32) < live_rows
    atom_dots = jnp.take(products, force_atom, axis=1)
    grad_dots = jnp.dot(sparse_panel, force_grad, preferred_element_type=jnp.float32)
    forces = jnp.where(keep_mask[None, :], atom_dots ** 3 * grad_dots, 0.0)
    kernel = jnp.concatenate([energy, forces], axis=1).astype(jnp.bfloat16)
    targets = jnp.concatenate([energy_target, jnp.where(keep_mask, force_target, jnp.zeros_like(force_target))])
    return kernel, targets


def reference(atom_desc, sparse_panel, atom_cell, energy_target, force_counts, force_atom, force_grad, force_target):
    def scan_step(totals, device):
        gram_sum, right_sum = totals
        kernel, targets = device_rows(
            sparse_panel,
            lax.dynamic_slice_in_dim(atom_desc, device * ATOMS_DEV, ATOMS_DEV, 1),
            lax.dynamic_slice_in_dim(atom_cell, device * ATOMS_DEV, ATOMS_DEV, 0),
            lax.dynamic_slice_in_dim(energy_target, device * CELLS_DEV, CELLS_DEV, 0),
            lax.dynamic_slice_in_dim(force_counts, device * CELLS_DEV, CELLS_DEV, 0),
            lax.dynamic_slice_in_dim(force_atom, device * FCAP, FCAP, 0),
            lax.dynamic_slice_in_dim(force_grad, device * FCAP, FCAP, 1),
            lax.dynamic_slice_in_dim(force_target, device * FCAP, FCAP, 0))
        gram_sum = gram_sum + lax.dot_general(kernel, kernel, (((1,), (1,)), ((), ())), preferred_element_type=jnp.float32)
        right_sum = right_sum + jnp.dot(kernel, targets, preferred_element_type=jnp.float32)
        return (gram_sum, right_sum), None

    start = (jnp.zeros((M, M), jnp.float32), jnp.zeros((M,), jnp.float32))
    (gram_sum, right_sum), unused = lax.scan(scan_step, start, jnp.arange(N_ROWS, dtype=jnp.int32))
    return gram_sum / ROWS_ALL, right_sum / ROWS_ALL
```

```python
import jax
import jax.numpy as jnp
from jax import lax
from jax.experimental import pallas as pl
from jax.experimental.pallas import tpu as pltpu
from jax.sharding import PartitionSpec as P

MESH = pl.DeviceIdType.MESH
F32, BF16 = jnp.float32, jnp.bfloat16
D, PTS, ATOMS, CELLS, SLOTS = 1000, 256, 512, 32, 1024
COLS = SLOTS + CELLS
ROWS_ALL = 34816.0
NN = (((1,), (0,)), ((), ()))
NT = (((1,), (1,)), ((), ()))


def dot(a, b, dims):
    return lax.dot_general(a, b, dims, preferred_element_type=F32)


def halves(value):
    high = value.astype(BF16)
    return high, (value - high.astype(F32)).astype(BF16)


def kernel(
    desc_hbm, panel_hbm, cell_ref, etarget_ref, counts_ref, fatom_ref, grad_hbm, ftarget_ref,
    gram_ref, right_ref,
    desc, grad, panel_t, panel, hot, member, kern, target, part1, recv1, part2, recv2,
    rpart, rz, rsum, ry,
    load_sem, x_send, x_recv, f_send, f_recv, d_send, d_recv, s1_send, s1_recv, s2_send, s2_recv,
    rz_send, rz_recv, ry_send, ry_recv, token,
):
    r, b = lax.axis_index("rows"), lax.axis_index("blk")
    z, y, x, c = r // 8, r % 8, b // 2, b % 2

    def dev(dz=0, dy=0, dx=0, dc=0):
        return ((z + dz) % 8) * 8 + (y + dy) % 8, ((x + dx) % 4) * 2 + (c + dc) % 2

    def remote(src, dst, send, recv, to):
        return pltpu.make_async_remote_copy(
            src_ref=src, dst_ref=dst, send_sem=send, recv_sem=recv, device_id=to, device_id_type=MESH
        )

    def arrived(ref, sem):
        pltpu.make_async_copy(ref, ref, sem).wait()

    partners = [dev(dc=1), dev(dx=2)]
    partners += [dev(dx=dx, dc=dc) for dx in (1, 3) for dc in (0, 1)]
    partners += [dev(dz=k) for k in range(1, 8)] + [dev(dy=k) for k in range(1, 8)]
    barrier = pltpu.get_barrier_semaphore()
    for partner in partners:
        pl.semaphore_signal(barrier, inc=1, device_id=partner, device_id_type=MESH)
    loads = [
        pltpu.make_async_copy(panel_hbm, panel_t, load_sem.at[0]),
        pltpu.make_async_copy(desc_hbm, desc, load_sem.at[1]),
        pltpu.make_async_copy(grad_hbm, grad, load_sem.at[2]),
    ]
    for load in loads:
        load.start()
    loads[0].wait()
    panel[0] = panel_t[...].T
    pl.semaphore_wait(barrier, len(partners))

    quarter = ((y + 2 * z) % 4) * 64
    sends = []
    for j in (1, 2):
        for h in (0, 1):
            rows = pl.ds(pl.multiple_of(quarter + 32 * h, 32), 32)
            copy = remote(panel.at[0, rows], panel.at[j, rows], x_send.at[j, h], x_recv.at[j, h], dev(dx=-j))
            copy.start()
            sends.append(copy)

    live = jnp.sum(counts_ref[...], axis=1, keepdims=True)
    keep = lax.broadcasted_iota(jnp.int32, (1, SLOTS), 1) < live
    slot_atom = jnp.where(keep, fatom_ref[...], -1)
    atoms = lax.broadcasted_iota(jnp.int32, (ATOMS, SLOTS), 0)
    hot[...] = jnp.where(atoms == slot_atom, 1.0, 0.0).astype(BF16)
    cells = lax.broadcasted_iota(jnp.int32, (CELLS, ATOMS), 0)
    member[...] = jnp.where(cells == cell_ref[...], 1.0, 0.0).astype(BF16)
    masked = jnp.where(keep, ftarget_ref[...].astype(F32), 0.0)
    target[:, :SLOTS] = jnp.broadcast_to(masked, (16, SLOTS)).astype(BF16)
    target[:, SLOTS:] = jnp.broadcast_to(etarget_ref[...].astype(F32), (16, CELLS)).astype(BF16)
    members = dot(jnp.ones((16, ATOMS), BF16), member[...], NT)[0:1]
    members = jnp.maximum(members, 1.0)
    loads[1].wait()
    loads[2].wait()

    def make_rows(j):
        points = panel[j]
        products = dot(points, desc[...], NN)
        high, low = halves(products)
        atom_dots = dot(high, hot[...], NN) + dot(low, hot[...], NN)
        grad_dots = dot(points, grad[...], NN)
        kern[j, c, :, :SLOTS] = (atom_dots * atom_dots * atom_dots * grad_dots).astype(BF16)
        squares = products * products
        high, low = halves(squares * squares)
        energy = dot(high, member[...], NT) + dot(low, member[...], NT)
        kern[j, c, :, SLOTS:] = (energy / members).astype(BF16)
        copy = remote(kern.at[j, c], kern.at[j, c], d_send.at[j], d_recv.at[j], dev(dc=1))
        copy.start()
        sends.append(copy)

    def multiply(j):
        arrived(kern.at[j, 1 - c], d_recv.at[j])
        for a in (0, 1):
            block = dot(kern[j, a], kern[0, c], NT).astype(BF16)
            if j < 2:
                for h in (0, 1):
                    for w in (0, 1):
                        part1[j, 4 * a + 2 * h + w] = block[128 * h : 128 * h + 128, 128 * w : 128 * w + 128]
            else:
                for q in range(8):
                    for w in (0, 1):
                        at = 32 * (2 * a + w)
                        part1[j, q, at : at + 32] = block[32 * q : 32 * q + 32, 128 * w : 128 * w + 128]
        for k in range(1, 8):
            if j < 2:
                to, piece = dev(dz=k), (z + k) % 8
            else:
                to, piece = dev(dy=k), (y + k) % 8
            copy = remote(part1.at[j, piece], recv1.at[j, k - 1], s1_send.at[j, k - 1], s1_recv.at[j], to)
            copy.start()
            sends.append(copy)

    def forward(j):
        for h in (0, 1):
            rows = pl.ds(pl.multiple_of(quarter + 32 * h, 32), 32)
            arrived(panel.at[j, rows], x_recv.at[j, h])
            for n, to in enumerate((dev(dy=1), dev(dy=-1), dev(dz=1 - 2 * h))):
                copy = remote(panel.at[j, rows], panel.at[j, rows], f_send.at[j, h, n], f_recv.at[j], to)
                copy.start()
                sends.append(copy)

    def gathered(j):
        rest = panel.at[j, pl.ds(0, 192)]
        arrived(rest, f_recv.at[j])

    make_rows(0)
    part = dot(target[...], kern[0, c], NT)[0:8]
    rpart[...] = part
    for k in range(1, 8):
        copy = remote(rpart, rz.at[k - 1], rz_send.at[k - 1], rz_recv, dev(dz=k))
        copy.start()
        sends.append(copy)
    multiply(0)
    forward(1)
    forward(2)
    gathered(1)
    make_rows(1)
    multiply(1)

    arrived(rz, rz_recv)
    total = jnp.zeros((8, PTS), F32)
    for s in range(8):
        slot = (z - s + 7) % 8
        value = rz[jnp.minimum(slot, 6)]
        total = total + jnp.where(slot == 7, part, value)
    rsum[...] = total
    for k in range(1, 8):
        copy = remote(rsum, ry.at[k - 1], ry_send.at[k - 1], ry_recv, dev(dy=k))
        copy.start()
        sends.append(copy)

    gathered(2)
    make_rows(2)
    multiply(2)

    arrived(ry, ry_recv)
    final = jnp.zeros((8, PTS), F32)
    for s in range(8):
        slot = (y - s + 7) % 8
        value = ry[jnp.minimum(slot, 6)]
        final = final + jnp.where(slot == 7, total, value)
    right_ref[...] = final[0:1] / ROWS_ALL
    for dc in (0, 1):
        pl.semaphore_signal(token, inc=1, device_id=dev(dx=-1, dc=dc), device_id_type=MESH)
    pl.semaphore_wait(token, 2)

    local = []

    def deliver(n, src, dst, to):
        here = (to[0] == r) & (to[1] == b)
        copy = remote(src, dst, s2_send.at[n], s2_recv, to)

        @pl.when(here)
        def _():
            pltpu.make_async_copy(src, dst, s2_recv).start()

        @pl.when(jnp.logical_not(here))
        def _():
            copy.start()

        local.append((here, copy))

    def first_sum(j, mine):
        arrived(recv1.at[j], s1_recv.at[j])
        acc = part1[j, mine].astype(F32)
        for k in range(7):
            acc = acc + recv1[j, k].astype(F32)
        return acc

    a, h, w = z // 4, (z // 2) % 2, z % 2
    for j in (0, 1):
        acc = first_sum(j, z)
        part2[j] = acc.astype(BF16)
        block = 2 * ((x + j) % 4) + a
        for k in range(4):
            src = part2.at[j, pl.ds(32 * k, 32)]
            deliver(4 * j + k, src, recv2.at[w, y], (block * 8 + 4 * h + k, b))
        if j == 1:
            part2[3] = acc.T.astype(BF16)
            for k in range(4):
                src = part2.at[3, pl.ds(32 * k, 32)]
                copy = remote(src, recv2.at[h, y], s2_send.at[12 + k], s2_recv, (b * 8 + 4 * w + k, block))
                copy.start()
                sends.append(copy)
    part2[2] = first_sum(2, y).astype(BF16)
    for a2 in (0, 1):
        for w2 in (0, 1):
            n = 2 * a2 + w2
            src = part2.at[2, pl.ds(32 * n, 32)]
            deliver(8 + n, src, recv2.at[w2, z], ((2 * ((x + 2) % 4) + a2) * 8 + y, b))

    arrived(recv2, s2_recv)
    for w2 in (0, 1):
        acc = recv2[w2, 0].astype(F32)
        for s in range(1, 8):
            acc = acc + recv2[w2, s].astype(F32)
        gram_ref[:, 128 * w2 : 128 * w2 + 128] = acc / ROWS_ALL

    for copy in sends:
        copy.wait_send()
    for here, copy in local:

        @pl.when(jnp.logical_not(here))
        def _(copy=copy):
            copy.wait_send()


def body(atom_desc, sparse_panel, atom_cell, energy_target, force_counts, force_atom, force_grad, force_target):
    vmem, any_ = pl.BlockSpec(memory_space=pltpu.VMEM), pl.BlockSpec(memory_space=pl.ANY)
    dma, sem = pltpu.VMEM, pltpu.SemaphoreType.DMA
    gram, right = pl.pallas_call(
        kernel,
        out_shape=(jax.ShapeDtypeStruct((32, PTS), F32), jax.ShapeDtypeStruct((1, PTS), F32)),
        in_specs=[any_, any_, vmem, vmem, vmem, vmem, any_, vmem],
        out_specs=(vmem, vmem),
        scratch_shapes=[
            dma((D, ATOMS), BF16),
            dma((D, SLOTS), BF16),
            dma((D, PTS), BF16),
            dma((3, PTS, D), BF16),
            dma((ATOMS, SLOTS), BF16),
            dma((CELLS, ATOMS), BF16),
            dma((3, 2, PTS, COLS), BF16),
            dma((16, COLS), BF16),
            dma((3, 8, 128, 128), BF16),
            dma((3, 7, 128, 128), BF16),
            dma((4, 128, 128), BF16),
            dma((2, 8, 32, 128), BF16),
            dma((8, PTS), F32),
            dma((7, 8, PTS), F32),
            dma((8, PTS), F32),
            dma((7, 8, PTS), F32),
            sem((3,)),
            sem((3, 2)),
            sem((3, 2)),
            sem((3, 2, 3)),
            sem((3,)),
            sem((3,)),
            sem((3,)),
            sem((3, 7)),
            sem((3,)),
            sem((16,)),
            sem,
            sem((7,)),
            sem,
            sem((7,)),
            sem,
            pltpu.SemaphoreType.REGULAR,
        ],
        compiler_params=pltpu.CompilerParams(
            collective_id=0, has_side_effects=True, vmem_limit_bytes=48 * 2**20
        ),
        name="gram",
    )(
        atom_desc,
        sparse_panel.T,
        atom_cell.reshape(1, ATOMS),
        energy_target.reshape(1, CELLS),
        force_counts.reshape(1, CELLS),
        force_atom.reshape(1, SLOTS),
        force_grad,
        force_target.reshape(1, SLOTS),
    )
    return gram, right.reshape(PTS)


def solution(mesh):
    in_specs = (
        P(None, "rows"),
        P("blk", None),
        P("rows"),
        P("rows"),
        P("rows"),
        P("rows"),
        P(None, "rows"),
        P("rows"),
    )
    out_specs = (P("rows", "blk"), P("blk"))
    return jax.shard_map(body, mesh=mesh, in_specs=in_specs, out_specs=out_specs, check_vma=False)
```

```python
import jax
import jax.numpy as jnp
from jax import lax
from jax.experimental import pallas as pl
from jax.experimental.pallas import tpu as pltpu
from jax.sharding import PartitionSpec as P

MESH = pl.DeviceIdType.MESH
F32, BF16 = jnp.float32, jnp.bfloat16
D, PTS, ATOMS, CELLS, SLOTS = 1000, 256, 512, 32, 1024
COLS = SLOTS + CELLS
ROWS_ALL = 34816.0
NN = (((1,), (0,)), ((), ()))
NT = (((1,), (1,)), ((), ()))


def dot(a, b, dims):
    return lax.dot_general(a, b, dims, preferred_element_type=F32)


def halves(value):
    high = value.astype(BF16)
    return high, (value - high.astype(F32)).astype(BF16)


def kernel(
    desc_hbm, panel_hbm, cell_hbm, etarget_hbm, counts_hbm, fatom_hbm, grad_hbm, ftarget_hbm,
    gram_ref, right_ref,
    desc, panel_t, cell_ref, etarget_ref, counts_ref, fatom_ref, grad, ftarget_ref,
    panel, hot, member, kern, target, part1, recv1, part2, recv2,
    rpart, rz, rsum, ry,
    load_sem, x_send, x_recv, f_send, f_recv, d_send, d_recv, s1_send, s1_recv, s2_send, s2_recv,
    rz_send, rz_recv, ry_send, ry_recv, token,
):
    r, b = lax.axis_index("rows"), lax.axis_index("blk")
    z, y, x, c = r // 8, r % 8, b // 2, b % 2

    def dev(dz=0, dy=0, dx=0, dc=0):
        return ((z + dz) % 8) * 8 + (y + dy) % 8, ((x + dx) % 4) * 2 + (c + dc) % 2

    def remote(src, dst, send, recv, to):
        return pltpu.make_async_remote_copy(
            src_ref=src, dst_ref=dst, send_sem=send, recv_sem=recv, device_id=to, device_id_type=MESH
        )

    def arrived(ref, sem):
        pltpu.make_async_copy(ref, ref, sem).wait()

    copies = (
        (panel_hbm, panel_t), (desc_hbm, desc), (grad_hbm, grad), (fatom_hbm, fatom_ref), (counts_hbm, counts_ref),
        (cell_hbm, cell_ref), (etarget_hbm, etarget_ref), (ftarget_hbm, ftarget_ref),
    )
    loads = [pltpu.make_async_copy(src, dst, load_sem.at[n]) for n, (src, dst) in enumerate(copies)]
    for load in loads:
        load.start()
    partners = [dev(dc=1), dev(dx=2)]
    partners += [dev(dx=dx, dc=dc) for dx in (1, 3) for dc in (0, 1)]
    partners += [dev(dz=k) for k in range(1, 8)] + [dev(dy=k) for k in range(1, 8)]
    barrier = pltpu.get_barrier_semaphore()
    for partner in partners:
        pl.semaphore_signal(barrier, inc=1, device_id=partner, device_id_type=MESH)
    loads[0].wait()
    points = panel_t[...].T
    panel[0] = points
    for p in range(8):
        for h in (0, 1):
            panel[3, 128 * h + 16 * p : 128 * h + 16 * p + 16] = points[32 * p + 16 * h : 32 * p + 16 * h + 16]

    for load in loads[3:]:
        load.wait()
    live = jnp.sum(counts_ref[...], axis=1, keepdims=True)
    keep = lax.broadcasted_iota(jnp.int32, (1, SLOTS), 1) < live
    slot_atom = jnp.where(keep, fatom_ref[...], -1)
    atoms = lax.broadcasted_iota(jnp.int32, (ATOMS, SLOTS), 0)
    hot[...] = jnp.where(atoms == slot_atom, 1.0, 0.0).astype(BF16)
    cells = lax.broadcasted_iota(jnp.int32, (CELLS, ATOMS), 0)
    member[...] = jnp.where(cells == cell_ref[...], 1.0, 0.0).astype(BF16)
    ftarget = ftarget_ref[...].astype(F32)
    ftarget = jnp.concatenate([ftarget[k : k + 1] for k in range(8)], axis=1)
    target[:, :SLOTS] = jnp.broadcast_to(jnp.where(keep, ftarget, 0.0), (16, SLOTS)).astype(BF16)
    target[:, SLOTS:] = jnp.broadcast_to(etarget_ref[...].astype(F32), (16, CELLS)).astype(BF16)
    members = dot(jnp.ones((16, ATOMS), BF16), member[...], NT)[0:1]
    members = jnp.maximum(members, 1.0)
    for load in loads[1:3]:
        load.wait()

    def make_rows(j, first, count):
        at, own = (0, c) if j == 0 else (1, j - 1)
        rows = slice(first, first + count)
        points = panel[j, rows]
        products = dot(points, desc[...], NN)
        high, low = halves(products)
        atom_dots = dot(high, hot[...], NN) + dot(low, hot[...], NN)
        grad_dots = dot(points, grad[...], NN)
        kern[at, own, rows, :SLOTS] = (atom_dots * atom_dots * atom_dots * grad_dots).astype(BF16)
        squares = products * products
        high, low = halves(squares * squares)
        energy = dot(high, member[...], NT) + dot(low, member[...], NT)
        kern[at, own, rows, SLOTS:] = (energy / members).astype(BF16)

    sends = []

    def send(src, dst, send_sem, recv_sem, to):
        copy = remote(src, dst, send_sem, recv_sem, to)
        copy.start()
        sends.append(copy)

    quarter = ((1 + c) * y + (2 - c) * z) % 4 * 32

    def share(h):
        return pl.ds(pl.multiple_of(128 * h + quarter, 32), 32)

    def fetch(j, h):
        src = panel.at[0 if j == 1 else 3, share(h)]
        send(src, panel.at[j, share(h)], x_send.at[j - 1, h], x_recv.at[j - 1, h], dev(dx=-j))

    def forward(j, h):
        block = panel.at[j, share(h)]
        arrived(block, x_recv.at[j - 1, h])
        side = 1 - 2 * h
        targets = (dev(dy=1 - c, dz=c), dev(dy=c - 1, dz=-c), dev(dy=c * side, dz=(1 - c) * side))
        for n, to in enumerate(targets):
            send(block, block, f_send.at[j - 1, h, n], f_recv.at[j - 1, h], to)

    def gathered(j, h):
        arrived(panel.at[j, pl.ds(128 * h, 96)], f_recv.at[j - 1, h])

    line = (1 - c) * z + c * y
    cross = c * z + (1 - c) * y

    def multiply(j, h):
        rows = kern[0, c, 128 * h : 128 * h + 128] if j == 0 else kern[1, j - 1, 128 * h : 128 * h + 128]
        for a in (0, 1):
            block = dot(rows, kern[0, a], NT).astype(BF16)
            for w in (0, 1):
                part = block[:, 128 * w : 128 * w + 128]
                if j < 2:
                    part1[j, 4 * h + 2 * a + w] = part
                else:
                    at = 64 * h + 16 * (2 * a + w)
                    for p in range(8):
                        part1[j, p, at : at + 16] = part[16 * p : 16 * p + 16]

    def step1(j):
        for k in range(1, 8):
            piece = (line + k) % 8
            to = dev(dz=(1 - c) * k, dy=c * k)
            send(part1.at[j, piece], recv1.at[j, k - 1], s1_send.at[j, k - 1], s1_recv.at[j], to)

    def step1_half(h):
        rows = pl.ds(64 * h, 64)
        for k in range(1, 8):
            src = part1.at[2, (y + k) % 8, rows]
            send(src, recv1.at[2, k - 1, rows], s1_send.at[2 + h, k - 1], s1_recv.at[2 + h], dev(dy=k))

    make_rows(0, 0, 256)
    part = dot(target[...], kern[0, c], NT)[0:8]
    rpart[...] = part
    pl.semaphore_wait(barrier, len(partners))
    fetch(1, 0)
    fetch(1, 1)
    send(kern.at[0, c], kern.at[0, c], d_send, d_recv, dev(dc=1))
    for k in range(1, 8):
        send(rpart, rz.at[k - 1], rz_send.at[k - 1], rz_recv, dev(dz=k))
    arrived(kern.at[0, 1 - c], d_recv)
    fetch(2, 0)
    fetch(2, 1)
    multiply(0, 0)
    multiply(0, 1)
    step1(0)
    forward(1, 0)
    forward(1, 1)
    forward(2, 0)
    gathered(1, 0)
    make_rows(1, 0, 128)
    forward(2, 1)
    gathered(1, 1)
    make_rows(1, 128, 128)
    multiply(1, 0)
    multiply(1, 1)
    step1(1)

    arrived(rz, rz_recv)
    total = jnp.zeros((8, PTS), F32)
    for s in range(8):
        slot = (z - s + 7) % 8
        value = rz[jnp.minimum(slot, 6)]
        total = total + jnp.where(slot == 7, part, value)
    rsum[...] = total
    for k in range(1, 8):
        send(rsum, ry.at[k - 1], ry_send.at[k - 1], ry_recv, dev(dy=k))

    for half in (0, 1):
        gathered(2, half)
        make_rows(2, 128 * half, 128)
        multiply(2, half)
        step1_half(half)

    arrived(ry, ry_recv)
    final = jnp.zeros((8, PTS), F32)
    for s in range(8):
        slot = (y - s + 7) % 8
        value = ry[jnp.minimum(slot, 6)]
        final = final + jnp.where(slot == 7, total, value)
    right_ref[...] = final[0:1] / ROWS_ALL
    for to in (dev(dc=1), dev(dx=-1), dev(dx=-1, dc=1)):
        pl.semaphore_signal(token, inc=1, device_id=to, device_id_type=MESH)
    pl.semaphore_wait(token, 3)

    local = []

    def deliver(n, src, dst, to):
        here = (to[0] == r) & (to[1] == b)
        copy = remote(src, dst, s2_send.at[n], s2_recv, to)

        @pl.when(here)
        def _():
            pltpu.make_async_copy(src, dst, s2_recv).start()

        @pl.when(jnp.logical_not(here))
        def _():
            copy.start()

        local.append((here, copy))

    def first_sum(j, mine, rows, sem):
        arrived(recv1.at[j, :, rows], sem)
        acc = part1[j, mine, rows].astype(F32)
        for k in range(7):
            acc = acc + recv1[j, k, rows].astype(F32)
        return acc

    h, a, w = line // 4, (line // 2) % 2, line % 2
    for j in (0, 1):
        acc = first_sum(j, line, pl.ds(0, 128), s1_recv.at[j])
        part2[j] = acc.astype(BF16)
        block = 2 * ((x + j) % 4) + c
        for k in range(4):
            src = part2.at[j, pl.ds(32 * k, 32)]
            deliver(4 * j + k, src, recv2.at[w, cross], (block * 8 + 4 * h + k, 2 * x + a))
        if j == 1:
            part2[3] = acc.T.astype(BF16)
            for k in range(4):
                src = part2.at[3, pl.ds(32 * k, 32)]
                to = ((2 * x + a) * 8 + 4 * w + k, block)
                send(src, recv2.at[h, cross], s2_send.at[16 + k], s2_recv, to)
    for half in (0, 1):
        rows = pl.ds(64 * half, 64)
        part2[2, rows] = first_sum(2, y, rows, s1_recv.at[2 + half]).astype(BF16)
        for n in range(4):
            src = part2.at[2, pl.ds(64 * half + 16 * n, 16)]
            dst = recv2.at[n % 2, z, pl.ds(16 * half, 16)]
            deliver(8 + 4 * half + n, src, dst, ((2 * ((x + 2) % 4) + c) * 8 + y, 2 * x + n // 2))

    arrived(recv2, s2_recv)
    for w2 in (0, 1):
        acc = recv2[w2, 0].astype(F32)
        for s in range(1, 8):
            acc = acc + recv2[w2, s].astype(F32)
        gram_ref[:, 128 * w2 : 128 * w2 + 128] = acc / ROWS_ALL

    for copy in sends:
        copy.wait_send()
    for here, copy in local:

        @pl.when(jnp.logical_not(here))
        def _(copy=copy):
            copy.wait_send()


def body(atom_desc, sparse_panel, atom_cell, energy_target, force_counts, force_atom, force_grad, force_target):
    vmem, hbm = pl.BlockSpec(memory_space=pltpu.VMEM), pl.BlockSpec(memory_space=pltpu.HBM)
    dma, sem = pltpu.VMEM, pltpu.SemaphoreType.DMA
    operands = (
        atom_desc,
        sparse_panel.T,
        atom_cell.reshape(1, ATOMS),
        energy_target.reshape(1, CELLS),
        force_counts.reshape(1, CELLS),
        force_atom.reshape(1, SLOTS),
        force_grad,
        force_target.reshape(8, 128),
    )
    gram, right = pl.pallas_call(
        kernel,
        out_shape=(jax.ShapeDtypeStruct((32, PTS), F32), jax.ShapeDtypeStruct((1, PTS), F32)),
        in_specs=[hbm] * 8,
        out_specs=(vmem, vmem),
        scratch_shapes=[
            dma((D, ATOMS), BF16),
            dma((D, PTS), BF16),
            dma((1, ATOMS), jnp.int32),
            dma((1, CELLS), BF16),
            dma((1, CELLS), jnp.int32),
            dma((1, SLOTS), jnp.int32),
            dma((D, SLOTS), BF16),
            dma((8, 128), BF16),
            dma((4, PTS, D), BF16),
            dma((ATOMS, SLOTS), BF16),
            dma((CELLS, ATOMS), BF16),
            dma((2, 2, PTS, COLS), BF16),
            dma((16, COLS), BF16),
            dma((3, 8, 128, 128), BF16),
            dma((3, 7, 128, 128), BF16),
            dma((4, 128, 128), BF16),
            dma((2, 8, 32, 128), BF16),
            dma((8, PTS), F32),
            dma((7, 8, PTS), F32),
            dma((8, PTS), F32),
            dma((7, 8, PTS), F32),
            sem((8,)),
            sem((2, 2)),
            sem((2, 2)),
            sem((2, 2, 3)),
            sem((2, 2)),
            sem,
            sem,
            sem((4, 7)),
            sem((4,)),
            sem((20,)),
            sem,
            sem((7,)),
            sem,
            sem((7,)),
            sem,
            pltpu.SemaphoreType.REGULAR,
        ],
        compiler_params=pltpu.CompilerParams(
            collective_id=0, has_side_effects=True, vmem_limit_bytes=24 * 2**20
        ),
        name="gram",
    )(*[pltpu.with_memory_space_constraint(operand, pltpu.HBM) for operand in operands])
    return gram, right.reshape(PTS)


def solution(mesh):
    in_specs = (
        P(None, "rows"),
        P("blk", None),
        P("rows"),
        P("rows"),
        P("rows"),
        P("rows"),
        P(None, "rows"),
        P("rows"),
    )
    out_specs = (P("rows", "blk"), P("blk"))
    return jax.shard_map(body, mesh=mesh, in_specs=in_specs, out_specs=out_specs, check_vma=False)
```

```python
import jax
import jax.numpy as jnp
from jax import lax
from jax.experimental import pallas as pl
from jax.experimental.pallas import tpu as pltpu
from jax.sharding import PartitionSpec as P

MESH = pl.DeviceIdType.MESH
F32, BF16 = jnp.float32, jnp.bfloat16
D, PTS, ATOMS, CELLS, SLOTS = 1000, 256, 512, 32, 1024
COLS = SLOTS + CELLS
ROWS_ALL = 34816.0
NN = (((1,), (0,)), ((), ()))
NT = (((1,), (1,)), ((), ()))


def dot(a, b, dims):
    return lax.dot_general(a, b, dims, preferred_element_type=F32)


def halves(value):
    high = value.astype(BF16)
    return high, (value - high.astype(F32)).astype(BF16)


def kernel(
    desc_hbm, panel_hbm, cell_hbm, etarget_hbm, counts_hbm, fatom_hbm, grad_hbm, ftarget_hbm,
    gram_ref, right_ref,
    desc, panel_t, cell_ref, etarget_ref, counts_ref, fatom_ref, grad, ftarget_ref,
    panel, hot, member, kern, target, part1, recv1, part2, recv2,
    rpart, rz, rsum, ry,
    load_sem, x_send, x_recv, f_send, f_recv, d_send, d_recv, s1_send, s1_recv, s2_send, s2_recv,
    rz_send, rz_recv, ry_send, ry_recv, token,
):
    r, b = lax.axis_index("rows"), lax.axis_index("blk")
    z, y, x, c = r // 8, r % 8, b // 2, b % 2

    def dev(dz=0, dy=0, dx=0, dc=0):
        return ((z + dz) % 8) * 8 + (y + dy) % 8, ((x + dx) % 4) * 2 + (c + dc) % 2

    def remote(src, dst, send, recv, to):
        return pltpu.make_async_remote_copy(
            src_ref=src, dst_ref=dst, send_sem=send, recv_sem=recv, device_id=to, device_id_type=MESH
        )

    def arrived(ref, sem):
        pltpu.make_async_copy(ref, ref, sem).wait()

    copies = (
        (panel_hbm, panel_t), (fatom_hbm, fatom_ref), (counts_hbm, counts_ref), (cell_hbm, cell_ref),
        (etarget_hbm, etarget_ref), (ftarget_hbm, ftarget_ref), (desc_hbm, desc), (grad_hbm, grad),
    )
    loads = [pltpu.make_async_copy(src, dst, load_sem.at[n]) for n, (src, dst) in enumerate(copies)]
    loads[0].start()
    around = [dev(dy=1), dev(dy=-1), dev(dz=1), dev(dz=-1)]
    partners = [dev(dc=1), dev(dx=2)] + [dev(dx=dx, dc=dc) for dx in (1, 3) for dc in (0, 1)] + around
    barrier = pltpu.get_barrier_semaphore()
    for partner in partners:
        pl.semaphore_signal(barrier, inc=1, device_id=partner, device_id_type=MESH)
    for load in loads[1:]:
        load.start()
    loads[0].wait()
    points = panel_t[...].T
    panel[0] = points
    for p in range(8):
        for h in (0, 1):
            panel[3, 128 * h + 16 * p : 128 * h + 16 * p + 16] = points[32 * p + 16 * h : 32 * p + 16 * h + 16]

    for load in loads[1:6]:
        load.wait()
    live = jnp.sum(counts_ref[...], axis=1, keepdims=True)
    keep = lax.broadcasted_iota(jnp.int32, (1, SLOTS), 1) < live
    slot_atom = jnp.where(keep, fatom_ref[...], -1)
    atoms = lax.broadcasted_iota(jnp.int32, (ATOMS, SLOTS), 0)
    hot[...] = jnp.where(atoms == slot_atom, 1.0, 0.0).astype(BF16)
    cells = lax.broadcasted_iota(jnp.int32, (CELLS, ATOMS), 0)
    member[...] = jnp.where(cells == cell_ref[...], 1.0, 0.0).astype(BF16)
    ftarget = ftarget_ref[...].astype(F32)
    ftarget = jnp.concatenate([ftarget[k : k + 1] for k in range(8)], axis=1)
    target[:, :SLOTS] = jnp.broadcast_to(jnp.where(keep, ftarget, 0.0), (16, SLOTS)).astype(BF16)
    target[:, SLOTS:] = jnp.broadcast_to(etarget_ref[...].astype(F32), (16, CELLS)).astype(BF16)
    members = dot(jnp.ones((16, ATOMS), BF16), member[...], NT)[0:1]
    members = jnp.maximum(members, 1.0)
    def make_rows(j, first, count):
        at, own = (0, c) if j == 0 else (1, j - 1)
        rows = slice(first, first + count)
        points = panel[j, rows]
        products = dot(points, desc[...], NN)
        high, low = halves(products)
        atom_dots = dot(high, hot[...], NN) + dot(low, hot[...], NN)
        grad_dots = dot(points, grad[...], NN)
        kern[at, own, rows, :SLOTS] = (atom_dots * atom_dots * atom_dots * grad_dots).astype(BF16)
        squares = products * products
        high, low = halves(squares * squares)
        energy = dot(high, member[...], NT) + dot(low, member[...], NT)
        kern[at, own, rows, SLOTS:] = (energy / members).astype(BF16)

    sends, local = [], []

    def send(src, dst, send_sem, recv_sem, to):
        copy = remote(src, dst, send_sem, recv_sem, to)
        copy.start()
        sends.append(copy)

    quarter = ((1 + c) * y + (2 - c) * z) % 4 * 32

    def share(h):
        return pl.ds(pl.multiple_of(128 * h + quarter, 32), 32)

    def fetch(j, h):
        src = panel.at[0 if j == 1 else 3, share(h)]
        send(src, panel.at[j, share(h)], x_send.at[j - 1, h], x_recv.at[j - 1, h], dev(dx=-j))

    def forward(j, h):
        block = panel.at[j, share(h)]
        arrived(block, x_recv.at[j - 1, h])
        side = 1 - 2 * h
        targets = (dev(dy=1 - c, dz=c), dev(dy=c - 1, dz=-c), dev(dy=c * side, dz=(1 - c) * side))
        for n, to in enumerate(targets):
            send(block, block, f_send.at[j - 1, h, n], f_recv.at[j - 1, h], to)

    def gathered(j, h):
        arrived(panel.at[j, pl.ds(128 * h, 96)], f_recv.at[j - 1, h])

    line = (1 - c) * z + c * y

    far_first = (4, 3, 5, 2, 6, 1, 7)

    def tell(n):
        for to in around:
            pl.semaphore_signal(token.at[n], inc=1, device_id=to, device_id_type=MESH)

    def hear(n):
        pl.semaphore_wait(token.at[n], len(around))

    def multiply_a():
        blocks = [dot(kern[0, c], kern[0, a], NT).astype(BF16) for a in (0, 1)]
        for core, pieces in enumerate((((0, 0), (0, 1), (0, 2), (1, 1), (1, 3)), ((0, 2), (0, 3), (0, 1), (1, 3), (1, 0)))):

            @pl.when(c == core)
            def _(pieces=pieces):
                for n, (h, w) in enumerate(pieces):
                    at = 128 * (w % 2)
                    part1[0, n] = blocks[w // 2][128 * h : 128 * h + 128, at : at + 128]

    def step1_a():
        for n in range(5):
            to = n + 3 * c
            k = (to - z + 8) % 8
            here = k == 0
            slot = jnp.where(here, 0, k - 1)
            copy = remote(part1.at[0, n], recv1.at[0, slot], s1_send.at[0, n], s1_recv.at[0], dev(dz=to - z + 8))

            @pl.when(jnp.logical_not(here))
            def _(copy=copy):
                copy.start()

            local.append((here, copy))

    def multiply_b():
        for a in (0, 1):
            block = dot(kern[1, 0], kern[0, a], NT).astype(BF16)
            for h in (0, 1):
                for w in (0, 1):
                    part1[1, 4 * w + 2 * h + a] = block[128 * h : 128 * h + 128, 128 * w : 128 * w + 128]

    def multiply_half(h):
        rows = kern[1, 1, 128 * h : 128 * h + 128]
        for a in (0, 1):
            block = dot(rows, kern[0, a], NT).astype(BF16)
            for w in (0, 1):
                at = 64 * h + 16 * (2 * a + w)
                for p in range(8):
                    part1[2, p, at : at + 16] = block[16 * p : 16 * p + 16, 128 * w : 128 * w + 128]

    def step1_b():
        for k in far_first:
            to = dev(dz=(1 - c) * k, dy=c * k)
            send(part1.at[1, (line + k) % 8], recv1.at[1, k - 1], s1_send.at[1, k - 1], s1_recv.at[1], to)

    def step1_half(h):
        rows = pl.ds(64 * h, 64)
        for k in far_first:
            src = part1.at[2, (y + k) % 8, rows]
            send(src, recv1.at[2, k - 1, rows], s1_send.at[2 + h, k - 1], s1_recv.at[2 + h], dev(dy=k))

    pl.semaphore_wait(barrier, len(partners))
    fetch(1, 0)
    fetch(1, 1)
    tell(0)
    for load in loads[6:]:
        load.wait()
    make_rows(0, 0, 256)
    send(kern.at[0, c], kern.at[0, c], d_send, d_recv, dev(dc=1))
    hear(0)
    tell(1)
    part = dot(target[...], kern[0, c], NT)[0:8]
    rpart[...] = part
    forward(1, 0)
    fetch(2, 0)
    fetch(2, 1)
    hear(1)
    tell(2)
    forward(1, 1)
    arrived(kern.at[0, 1 - c], d_recv)
    multiply_a()
    hear(2)
    for k in far_first:
        send(rpart, rz.at[k - 1], rz_send.at[k - 1], rz_recv, dev(dz=k))
    forward(2, 0)
    gathered(1, 0)
    make_rows(1, 0, 128)
    forward(2, 1)
    step1_a()
    gathered(1, 1)
    make_rows(1, 128, 128)
    multiply_b()
    step1_b()

    gathered(2, 0)
    make_rows(2, 0, 128)
    multiply_half(0)
    step1_half(0)

    arrived(rz, rz_recv)
    for to in (dev(dc=1), dev(dx=-1), dev(dx=-1, dc=1)):
        pl.semaphore_signal(token.at[3], inc=1, device_id=to, device_id_type=MESH)
    total = jnp.zeros((8, PTS), F32)
    for s in range(8):
        slot = (z - s + 7) % 8
        value = rz[jnp.minimum(slot, 6)]
        total = total + jnp.where(slot == 7, part, value)
    rsum[...] = total
    for k in far_first:
        send(rsum, ry.at[k - 1], ry_send.at[k - 1], ry_recv, dev(dy=k))

    gathered(2, 1)
    make_rows(2, 128, 128)
    multiply_half(1)
    step1_half(1)

    pl.semaphore_wait(token.at[3], 3)

    def deliver(n, src, dst, to):
        here = (to[0] == r) & (to[1] == b)
        copy = remote(src, dst, s2_send.at[n], s2_recv, to)

        @pl.when(here)
        def _():
            pltpu.make_async_copy(src, dst, s2_recv).start()

        @pl.when(jnp.logical_not(here))
        def _():
            copy.start()

        return here, copy

    def first_sum(j, mine, rows, sem):
        arrived(recv1.at[j, :, rows], sem)
        acc = part1[j, mine, rows].astype(F32)
        for k in range(7):
            acc = acc + recv1[j, k, rows].astype(F32)
        return acc

    n = z - 3 * c
    down = 2 * c + jnp.where(n >= 3, 1, 0)
    first = jnp.where(n == 3, 1, jnp.where(n == 4, 3, n))
    second = jnp.where(n == 0, 2, jnp.where(n == 2, 1, jnp.where(n == 4, 0, 3)))
    across = jnp.where(c == 0, first, second)

    holds = (n >= 0) & (n < 5)
    targets_a = [((2 * x + down // 2) * 8 + 4 * (down % 2) + k, 2 * x + across // 2) for k in range(4)]
    targets_t = [((2 * x + across // 2) * 8 + 4 * (across % 2) + k, 2 * x + down // 2) for k in range(4)]

    @pl.when(holds)
    def _():
        acc = first_sum(0, n, pl.ds(0, 128), s1_recv.at[0])
        part2[0] = acc.astype(BF16)
        for k in range(4):
            src = part2.at[0, pl.ds(32 * k, 32)]
            deliver(8 + k, src, recv2.at[across % 2, y], targets_a[k])

        @pl.when(down != across)
        def _():
            part2[4] = acc.T.astype(BF16)
            for k in range(4):
                src = part2.at[4, pl.ds(32 * k, 32)]
                deliver(12 + k, src, recv2.at[down % 2, y], targets_t[k])

    w, h, a = line // 4, (line // 2) % 2, line % 2
    cross, block = z + y - line, 2 * ((x + 1) % 4) + c
    acc = first_sum(1, line, pl.ds(0, 128), s1_recv.at[1])
    part2[1] = acc.astype(BF16)
    part2[3] = acc.T.astype(BF16)
    for k in range(4):
        src = part2.at[3, pl.ds(32 * k, 32)]
        send(src, recv2.at[h, cross], s2_send.at[k], s2_recv, ((2 * x + a) * 8 + 4 * w + k, block))
    for k in range(4):
        src = part2.at[1, pl.ds(32 * k, 32)]
        local.append(deliver(4 + k, src, recv2.at[w, cross], (block * 8 + 4 * h + k, 2 * x + a)))

    for half in (0, 1):
        rows = pl.ds(64 * half, 64)
        part2[2, rows] = first_sum(2, y, rows, s1_recv.at[2 + half]).astype(BF16)
        for n in range(4):
            src = part2.at[2, pl.ds(64 * half + 16 * n, 16)]
            dst = recv2.at[n % 2, z, pl.ds(16 * half, 16)]
            to = ((2 * ((x + 2) % 4) + c) * 8 + y, 2 * x + n // 2)
            local.append(deliver(16 + 4 * half + n, src, dst, to))

    arrived(ry, ry_recv)
    final = jnp.zeros((8, PTS), F32)
    for s in range(8):
        slot = (y - s + 7) % 8
        value = ry[jnp.minimum(slot, 6)]
        final = final + jnp.where(slot == 7, total, value)
    right_ref[...] = final[0:1] / ROWS_ALL

    for k in range(4):
        for n, src, to, active in ((8, 0, targets_a[k], holds), (12, 4, targets_t[k], holds & (down != across))):
            here = (to[0] == r) & (to[1] == b)
            copy = remote(part2.at[src, pl.ds(32 * k, 32)], recv2.at[0, 0], s2_send.at[n + k], s2_recv, to)
            local.append((here | jnp.logical_not(active), copy))
    for copy in sends:
        copy.wait_send()
    for here, copy in local:

        @pl.when(jnp.logical_not(here))
        def _(copy=copy):
            copy.wait_send()

    arrived(recv2, s2_recv)
    for w2 in (0, 1):
        acc = recv2[w2, 0].astype(F32)
        for s in range(1, 8):
            acc = acc + recv2[w2, s].astype(F32)
        gram_ref[:, 128 * w2 : 128 * w2 + 128] = acc / ROWS_ALL


def body(atom_desc, sparse_panel, atom_cell, energy_target, force_counts, force_atom, force_grad, force_target):
    vmem, hbm = pl.BlockSpec(memory_space=pltpu.VMEM), pl.BlockSpec(memory_space=pltpu.HBM)
    dma, sem = pltpu.VMEM, pltpu.SemaphoreType.DMA
    operands = (
        atom_desc,
        sparse_panel.T,
        atom_cell.reshape(1, ATOMS),
        energy_target.reshape(1, CELLS),
        force_counts.reshape(1, CELLS),
        force_atom.reshape(1, SLOTS),
        force_grad,
        force_target.reshape(8, 128),
    )
    gram, right = pl.pallas_call(
        kernel,
        out_shape=(jax.ShapeDtypeStruct((32, PTS), F32), jax.ShapeDtypeStruct((1, PTS), F32)),
        in_specs=[hbm] * 8,
        out_specs=(vmem, vmem),
        scratch_shapes=[
            dma((D, ATOMS), BF16),
            dma((D, PTS), BF16),
            dma((1, ATOMS), jnp.int32),
            dma((1, CELLS), BF16),
            dma((1, CELLS), jnp.int32),
            dma((1, SLOTS), jnp.int32),
            dma((D, SLOTS), BF16),
            dma((8, 128), BF16),
            dma((4, PTS, D), BF16),
            dma((ATOMS, SLOTS), BF16),
            dma((CELLS, ATOMS), BF16),
            dma((2, 2, PTS, COLS), BF16),
            dma((16, COLS), BF16),
            dma((3, 8, 128, 128), BF16),
            dma((3, 7, 128, 128), BF16),
            dma((5, 128, 128), BF16),
            dma((2, 8, 32, 128), BF16),
            dma((8, PTS), F32),
            dma((7, 8, PTS), F32),
            dma((8, PTS), F32),
            dma((7, 8, PTS), F32),
            sem((8,)),
            sem((2, 2)),
            sem((2, 2)),
            sem((2, 2, 3)),
            sem((2, 2)),
            sem,
            sem,
            sem((4, 7)),
            sem((4,)),
            sem((24,)),
            sem,
            sem((7,)),
            sem,
            sem((7,)),
            sem,
            pltpu.SemaphoreType.REGULAR((4,)),
        ],
        compiler_params=pltpu.CompilerParams(
            collective_id=0, has_side_effects=True, vmem_limit_bytes=24 * 2**20
        ),
        name="gram",
    )(*[pltpu.with_memory_space_constraint(operand, pltpu.HBM) for operand in operands])
    return gram, right.reshape(PTS)


def solution(mesh):
    in_specs = (
        P(None, "rows"),
        P("blk", None),
        P("rows"),
        P("rows"),
        P("rows"),
        P("rows"),
        P(None, "rows"),
        P("rows"),
    )
    out_specs = (P("rows", "blk"), P("blk"))
    return jax.shard_map(body, mesh=mesh, in_specs=in_specs, out_specs=out_specs, check_vma=False)
```

```python
import jax
import jax.numpy as jnp
from jax import lax
from jax.experimental import pallas as pl
from jax.experimental.pallas import tpu as pltpu
from jax.sharding import PartitionSpec as P

MESH = pl.DeviceIdType.MESH
F32, BF16 = jnp.float32, jnp.bfloat16
D, PTS, ATOMS, CELLS, SLOTS = 1000, 256, 512, 32, 1024
COLS = SLOTS + CELLS
ROWS_ALL = 34816.0
NN = (((1,), (0,)), ((), ()))
NT = (((1,), (1,)), ((), ()))


def dot(a, b, dims):
    return lax.dot_general(a, b, dims, preferred_element_type=F32)


def halves(value):
    high = value.astype(BF16)
    return high, (value - high.astype(F32)).astype(BF16)


def kernel(
    desc_hbm, panel_hbm, cell_hbm, etarget_hbm, counts_hbm, fatom_hbm, grad_hbm, ftarget_hbm,
    gram_ref, right_ref,
    desc, panel_t, cell_ref, etarget_ref, counts_ref, fatom_ref, grad, ftarget_ref,
    panel, hot, member, kern, target, part1, recv1, part2, recv2,
    rpart, rz, rsum, ry,
    load_sem, x_send, x_recv, f_send, f_recv, d_send, d_recv, s1_send, s1_recv, s2_send, s2_recv,
    rz_send, rz_recv, ry_send, ry_recv, token,
):
    r, b = lax.axis_index("rows"), lax.axis_index("blk")
    z, y, x, c = r // 8, r % 8, b // 2, b % 2

    def dev(dz=0, dy=0, dx=0, dc=0):
        return ((z + dz) % 8) * 8 + (y + dy) % 8, ((x + dx) % 4) * 2 + (c + dc) % 2

    def remote(src, dst, send, recv, to):
        return pltpu.make_async_remote_copy(
            src_ref=src, dst_ref=dst, send_sem=send, recv_sem=recv, device_id=to, device_id_type=MESH
        )

    def arrived(ref, sem):
        pltpu.make_async_copy(ref, ref, sem).wait()

    copies = (
        (panel_hbm, panel_t), (fatom_hbm, fatom_ref), (counts_hbm, counts_ref), (cell_hbm, cell_ref),
        (etarget_hbm, etarget_ref), (ftarget_hbm, ftarget_ref), (desc_hbm, desc), (grad_hbm, grad),
    )
    loads = [pltpu.make_async_copy(src, dst, load_sem.at[n]) for n, (src, dst) in enumerate(copies)]
    loads[0].start()
    around = [dev(dy=1), dev(dy=-1), dev(dz=1), dev(dz=-1)]
    partners = [dev(dc=1), dev(dx=2)] + [dev(dx=dx, dc=dc) for dx in (1, 3) for dc in (0, 1)] + around
    barrier = pltpu.get_barrier_semaphore()
    for partner in partners:
        pl.semaphore_signal(barrier, inc=1, device_id=partner, device_id_type=MESH)
    for load in loads[1:]:
        load.start()
    loads[0].wait()
    points = panel_t[...].T
    panel[0] = points
    for p in range(8):
        for h in (0, 1):
            panel[3, 128 * h + 16 * p : 128 * h + 16 * p + 16] = points[32 * p + 16 * h : 32 * p + 16 * h + 16]

    for load in loads[1:6]:
        load.wait()
    live = jnp.sum(counts_ref[...], axis=1, keepdims=True)
    keep = lax.broadcasted_iota(jnp.int32, (1, SLOTS), 1) < live
    slot_atom = jnp.where(keep, fatom_ref[...], -1)
    atoms = lax.broadcasted_iota(jnp.int32, (ATOMS, SLOTS), 0)
    hot[...] = jnp.where(atoms == slot_atom, 1.0, 0.0).astype(BF16)
    cells = lax.broadcasted_iota(jnp.int32, (CELLS, ATOMS), 0)
    member[...] = jnp.where(cells == cell_ref[...], 1.0, 0.0).astype(BF16)
    ftarget = ftarget_ref[...].astype(F32)
    ftarget = jnp.concatenate([ftarget[k : k + 1] for k in range(8)], axis=1)
    target[:, :SLOTS] = jnp.broadcast_to(jnp.where(keep, ftarget, 0.0), (16, SLOTS)).astype(BF16)
    target[:, SLOTS:] = jnp.broadcast_to(etarget_ref[...].astype(F32), (16, CELLS)).astype(BF16)
    members = dot(jnp.ones((16, ATOMS), BF16), member[...], NT)[0:1]
    members = jnp.maximum(members, 1.0)
    def make_rows(j, first, count):
        at, own = (0, c) if j == 0 else (1, j - 1)
        rows = slice(first, first + count)
        points = panel[j, rows]
        products = dot(points, desc[...], NN)
        high, low = halves(products)
        atom_dots = dot(high, hot[...], NN) + dot(low, hot[...], NN)
        grad_dots = dot(points, grad[...], NN)
        kern[at, own, rows, :SLOTS] = (atom_dots * atom_dots * atom_dots * grad_dots).astype(BF16)
        squares = products * products
        high, low = halves(squares * squares)
        energy = dot(high, member[...], NT) + dot(low, member[...], NT)
        kern[at, own, rows, SLOTS:] = (energy / members).astype(BF16)

    def send(src, dst, send_sem, recv_sem, to):
        remote(src, dst, send_sem, recv_sem, to).start()

    quarter = ((1 + c) * y + (2 - c) * z) % 4 * 32

    def share(h):
        return pl.ds(pl.multiple_of(128 * h + quarter, 32), 32)

    def fetch(j, h):
        src = panel.at[0 if j == 1 else 3, share(h)]
        send(src, panel.at[j, share(h)], x_send, x_recv.at[j - 1, h], dev(dx=-j))

    def fetch_c(now):
        @pl.when(now)
        def _():
            fetch(2, 0)
            fetch(2, 1)

    def forward(j, h):
        block = panel.at[j, share(h)]
        arrived(block, x_recv.at[j - 1, h])
        side = 1 - 2 * h
        targets = (dev(dy=1 - c, dz=c), dev(dy=c - 1, dz=-c), dev(dy=c * side, dz=(1 - c) * side))
        for to in targets:
            send(block, block, f_send, f_recv.at[j - 1, h], to)

    def gathered(j, h):
        arrived(panel.at[j, pl.ds(128 * h, 96)], f_recv.at[j - 1, h])

    line = (1 - c) * z + c * y

    far_first = (4, 3, 5, 2, 6, 1, 7)

    def tell(n):
        for to in around:
            pl.semaphore_signal(token.at[n], inc=1, device_id=to, device_id_type=MESH)

    def hear(n):
        pl.semaphore_wait(token.at[n], len(around))

    def multiply_a():
        blocks = [dot(kern[0, c], kern[0, a], NT).astype(BF16) for a in (0, 1)]
        for core, pieces in enumerate((((0, 0), (0, 1), (0, 2), (1, 1), (1, 3)), ((0, 2), (0, 3), (0, 1), (1, 3), (1, 0)))):

            @pl.when(c == core)
            def _(pieces=pieces):
                for n, (h, w) in enumerate(pieces):
                    at = 128 * (w % 2)
                    part1[0, n] = blocks[w // 2][128 * h : 128 * h + 128, at : at + 128]

    def step1_a(now):
        for n in range(5):
            to = n + 3 * c
            k = (to - z + 8) % 8
            here = k == 0
            slot = jnp.where(here, 0, k - 1)
            copy = remote(part1.at[0, n], recv1.at[0, slot], s1_send.at[0], s1_recv.at[0], dev(dz=to - z + 8))

            @pl.when(jnp.logical_not(here) & now)
            def _(copy=copy):
                copy.start()

    def multiply_b():
        for a in (0, 1):
            block = dot(kern[1, 0], kern[0, a], NT).astype(BF16)
            for h in (0, 1):
                for w in (0, 1):
                    part1[1, 4 * w + 2 * h + a] = block[128 * h : 128 * h + 128, 128 * w : 128 * w + 128]

    def multiply_half(h):
        rows = kern[1, 1, 128 * h : 128 * h + 128]
        for a in (0, 1):
            block = dot(rows, kern[0, a], NT).astype(BF16)
            for w in (0, 1):
                at = 64 * h + 16 * (2 * a + w)
                for p in range(8):
                    part1[2, p, at : at + 16] = block[16 * p : 16 * p + 16, 128 * w : 128 * w + 128]

    def step1_b(now):
        @pl.when(now)
        def _():
            for k in far_first:
                to = dev(dz=(1 - c) * k, dy=c * k)
                send(part1.at[1, (line + k) % 8], recv1.at[1, k - 1], s1_send.at[1], s1_recv.at[1], to)

    def step1_half(h):
        rows = pl.ds(64 * h, 64)
        for k in far_first:
            src = part1.at[2, (y + k) % 8, rows]
            send(src, recv1.at[2, k - 1, rows], s1_send.at[2], s1_recv.at[2 + h], dev(dy=k))

    pl.semaphore_wait(barrier, len(partners))
    fetch(1, 0)
    fetch(1, 1)
    tell(0)
    for load in loads[6:]:
        load.wait()
    make_rows(0, 0, 256)
    send(kern.at[0, c], kern.at[0, c], d_send, d_recv, dev(dc=1))
    hear(0)
    tell(1)
    part = dot(target[...], kern[0, c], NT)[0:8]
    rpart[...] = part
    forward(1, 0)
    fetch_c(x != 1)
    hear(1)
    tell(2)
    forward(1, 1)
    fetch_c(x == 1)
    arrived(kern.at[0, 1 - c], d_recv)
    multiply_a()
    hear(2)
    for k in far_first:
        send(rpart, rz.at[k - 1], rz_send, rz_recv, dev(dz=k))
    forward(2, 0)
    gathered(1, 0)
    make_rows(1, 0, 128)
    forward(2, 1)
    step1_a(x < 2)
    gathered(1, 1)
    make_rows(1, 128, 128)
    multiply_b()
    step1_b(x != 2)

    gathered(2, 0)
    make_rows(2, 0, 128)
    multiply_half(0)
    step1_half(0)

    arrived(rz, rz_recv)
    for to in (dev(dc=1), dev(dx=-1), dev(dx=-1, dc=1)):
        pl.semaphore_signal(token.at[3], inc=1, device_id=to, device_id_type=MESH)
    total = jnp.zeros((8, PTS), F32)
    for s in range(8):
        slot = (z - s + 7) % 8
        value = rz[jnp.minimum(slot, 6)]
        total = total + jnp.where(slot == 7, part, value)
    rsum[...] = total
    for k in far_first:
        send(rsum, ry.at[k - 1], ry_send, ry_recv, dev(dy=k))

    gathered(2, 1)
    make_rows(2, 128, 128)
    multiply_half(1)
    step1_half(1)
    step1_b(x == 2)
    step1_a(x >= 2)

    pl.semaphore_wait(token.at[3], 3)

    def deliver(n, src, dst, to):
        here = (to[0] == r) & (to[1] == b)

        @pl.when(here)
        def _():
            pltpu.make_async_copy(src, dst, s2_recv).start()

        @pl.when(jnp.logical_not(here))
        def _():
            send(src, dst, s2_send.at[n], s2_recv, to)

    def first_sum(j, mine, rows, sem):
        arrived(recv1.at[j, :, rows], sem)
        acc = part1[j, mine, rows].astype(F32)
        for k in range(7):
            acc = acc + recv1[j, k, rows].astype(F32)
        return acc

    n = z - 3 * c
    down = 2 * c + jnp.where(n >= 3, 1, 0)
    first = jnp.where(n == 3, 1, jnp.where(n == 4, 3, n))
    second = jnp.where(n == 0, 2, jnp.where(n == 2, 1, jnp.where(n == 4, 0, 3)))
    across = jnp.where(c == 0, first, second)

    holds = (n >= 0) & (n < 5)
    targets_a = [((2 * x + down // 2) * 8 + 4 * (down % 2) + k, 2 * x + across // 2) for k in range(4)]
    targets_t = [((2 * x + across // 2) * 8 + 4 * (across % 2) + k, 2 * x + down // 2) for k in range(4)]

    def step2_a(now):
        @pl.when(holds & now)
        def _():
            acc = first_sum(0, n, pl.ds(0, 128), s1_recv.at[0])
            part2[0] = acc.astype(BF16)
            for k in range(4):
                src = part2.at[0, pl.ds(32 * k, 32)]
                deliver(0, src, recv2.at[across % 2, y], targets_a[k])

            @pl.when(down != across)
            def _():
                part2[4] = acc.T.astype(BF16)
                for k in range(4):
                    src = part2.at[4, pl.ds(32 * k, 32)]
                    deliver(1, src, recv2.at[down % 2, y], targets_t[k])

    w, h, a = line // 4, (line // 2) % 2, line % 2
    cross, block = z + y - line, 2 * ((x + 1) % 4) + c

    def step2_b(now):
        @pl.when(now)
        def _():
            acc = first_sum(1, line, pl.ds(0, 128), s1_recv.at[1])
            part2[1] = acc.astype(BF16)
            part2[3] = acc.T.astype(BF16)
            for k in range(4):
                src = part2.at[3, pl.ds(32 * k, 32)]
                send(src, recv2.at[h, cross], s2_send.at[2], s2_recv, ((2 * x + a) * 8 + 4 * w + k, block))
            for k in range(4):
                src = part2.at[1, pl.ds(32 * k, 32)]
                deliver(3, src, recv2.at[w, cross], (block * 8 + 4 * h + k, 2 * x + a))

    def step2_c():
        for half in (0, 1):
            rows = pl.ds(64 * half, 64)
            part2[2, rows] = first_sum(2, y, rows, s1_recv.at[2 + half]).astype(BF16)
            for n in range(4):
                src = part2.at[2, pl.ds(64 * half + 16 * n, 16)]
                dst = recv2.at[n % 2, z, pl.ds(16 * half, 16)]
                to = ((2 * ((x + 2) % 4) + c) * 8 + y, 2 * x + n // 2)
                deliver(4, src, dst, to)

    step2_a(x < 2)
    step2_b(x != 2)
    step2_c()
    step2_b(x == 2)
    step2_a(x >= 2)

    arrived(ry, ry_recv)
    final = jnp.zeros((8, PTS), F32)
    for s in range(8):
        slot = (y - s + 7) % 8
        value = ry[jnp.minimum(slot, 6)]
        final = final + jnp.where(slot == 7, total, value)
    right_ref[...] = final[0:1] / ROWS_ALL

    arrived(panel.at[0, pl.ds(0, 128)], x_send)
    arrived(panel.at[pl.ds(0, 3), pl.ds(0, 128)], f_send)
    arrived(kern.at[0, c], d_send)
    arrived(rz, rz_send)
    arrived(ry, ry_send)
    arrived(recv1.at[1], s1_send.at[1])
    arrived(recv1.at[2], s1_send.at[2])
    arrived(part2.at[2], s2_send.at[2])

    def left(ref, few, many, fewer, sem, active=True):
        @pl.when(active & fewer)
        def _():
            arrived(ref.at[pl.ds(0, few)], sem)

        @pl.when(active & jnp.logical_not(fewer))
        def _():
            arrived(ref.at[pl.ds(0, many)], sem)

    def among(targets):
        found = False
        for to in targets:
            found = found | ((to[0] == r) & (to[1] == b))
        return found

    flat = part2.at[0]
    left(recv1.at[0], 4, 5, holds, s1_send.at[0])
    left(flat, 96, 128, among(targets_a), s2_send.at[0], holds)
    left(flat, 96, 128, among(targets_t), s2_send.at[1], holds & (down != across))
    left(flat, 96, 128, among([(block * 8 + 4 * h + k, 2 * x + a) for k in range(4)]), s2_send.at[3])
    left(flat, 64, 128, z == 2 * ((x + 2) % 4) + c, s2_send.at[4])

    arrived(recv2, s2_recv)
    for w2 in (0, 1):
        acc = recv2[w2, 0].astype(F32)
        for s in range(1, 8):
            acc = acc + recv2[w2, s].astype(F32)
        gram_ref[:, 128 * w2 : 128 * w2 + 128] = acc / ROWS_ALL


def body(atom_desc, sparse_panel, atom_cell, energy_target, force_counts, force_atom, force_grad, force_target):
    vmem, hbm = pl.BlockSpec(memory_space=pltpu.VMEM), pl.BlockSpec(memory_space=pltpu.HBM)
    dma, sem = pltpu.VMEM, pltpu.SemaphoreType.DMA
    operands = (
        atom_desc,
        sparse_panel.T,
        atom_cell.reshape(1, ATOMS),
        energy_target.reshape(1, CELLS),
        force_counts.reshape(1, CELLS),
        force_atom.reshape(1, SLOTS),
        force_grad,
        force_target.reshape(8, 128),
    )
    gram, right = pl.pallas_call(
        kernel,
        out_shape=(jax.ShapeDtypeStruct((32, PTS), F32), jax.ShapeDtypeStruct((1, PTS), F32)),
        in_specs=[hbm] * 8,
        out_specs=(vmem, vmem),
        scratch_shapes=[
            dma((D, ATOMS), BF16),
            dma((D, PTS), BF16),
            dma((1, ATOMS), jnp.int32),
            dma((1, CELLS), BF16),
            dma((1, CELLS), jnp.int32),
            dma((1, SLOTS), jnp.int32),
            dma((D, SLOTS), BF16),
            dma((8, 128), BF16),
            dma((4, PTS, D), BF16),
            dma((ATOMS, SLOTS), BF16),
            dma((CELLS, ATOMS), BF16),
            dma((2, 2, PTS, COLS), BF16),
            dma((16, COLS), BF16),
            dma((3, 8, 128, 128), BF16),
            dma((3, 7, 128, 128), BF16),
            dma((5, 128, 128), BF16),
            dma((2, 8, 32, 128), BF16),
            dma((8, PTS), F32),
            dma((7, 8, PTS), F32),
            dma((8, PTS), F32),
            dma((7, 8, PTS), F32),
            sem((8,)),
            sem,
            sem((2, 2)),
            sem,
            sem((2, 2)),
            sem,
            sem,
            sem((3,)),
            sem((4,)),
            sem((5,)),
            sem,
            sem,
            sem,
            sem,
            sem,
            pltpu.SemaphoreType.REGULAR((4,)),
        ],
        compiler_params=pltpu.CompilerParams(
            collective_id=0, has_side_effects=True, vmem_limit_bytes=24 * 2**20
        ),
        name="gram",
    )(*[pltpu.with_memory_space_constraint(operand, pltpu.HBM) for operand in operands])
    return gram, right.reshape(PTS)


def solution(mesh):
    in_specs = (
        P(None, "rows"),
        P("blk", None),
        P("rows"),
        P("rows"),
        P("rows"),
        P("rows"),
        P(None, "rows"),
        P("rows"),
    )
    out_specs = (P("rows", "blk"), P("blk"))
    return jax.shard_map(body, mesh=mesh, in_specs=in_specs, out_specs=out_specs, check_vma=False)
```

```python
import jax
import jax.numpy as jnp
from jax import lax
from jax.experimental import pallas as pl
from jax.experimental.pallas import tpu as pltpu
from jax.sharding import PartitionSpec as P

MESH = pl.DeviceIdType.MESH
F32, BF16 = jnp.float32, jnp.bfloat16
D, PTS, ATOMS, CELLS, SLOTS = 1000, 256, 512, 32, 1024
COLS = SLOTS + CELLS
ROWS_ALL = 34816.0
NN = (((1,), (0,)), ((), ()))
NT = (((1,), (1,)), ((), ()))


def dot(a, b, dims):
    return lax.dot_general(a, b, dims, preferred_element_type=F32)


def halves(value):
    high = value.astype(BF16)
    return high, (value - high.astype(F32)).astype(BF16)


def kernel(
    desc_hbm, panel_hbm, cell_hbm, etarget_hbm, counts_hbm, fatom_hbm, grad_hbm, ftarget_hbm,
    gram_ref, right_ref,
    desc, panel_t, cell_ref, etarget_ref, counts_ref, fatom_ref, grad, ftarget_ref,
    panel, hot, member, kern, target, part1, recv1, part2, recv2,
    rpart, rz, rsum, ry,
    load_sem, x_send, x_recv, f_send, f_recv, d_send, d_recv, s1_send, s1_recv, s2_send, s2_recv,
    rz_send, rz_recv, ry_send, ry_recv, token,
):
    r, b = lax.axis_index("rows"), lax.axis_index("blk")
    z, y, x, c = r // 8, r % 8, b // 2, b % 2

    def dev(dz=0, dy=0, dx=0, dc=0):
        return ((z + dz) % 8) * 8 + (y + dy) % 8, ((x + dx) % 4) * 2 + (c + dc) % 2

    def remote(src, dst, send, recv, to):
        return pltpu.make_async_remote_copy(
            src_ref=src, dst_ref=dst, send_sem=send, recv_sem=recv, device_id=to, device_id_type=MESH
        )

    def arrived(ref, sem):
        pltpu.make_async_copy(ref, ref, sem).wait()

    copies = (
        (panel_hbm, panel_t), (fatom_hbm, fatom_ref), (counts_hbm, counts_ref), (cell_hbm, cell_ref),
        (etarget_hbm, etarget_ref), (ftarget_hbm, ftarget_ref), (desc_hbm, desc), (grad_hbm, grad),
    )
    loads = [pltpu.make_async_copy(src, dst, load_sem.at[n]) for n, (src, dst) in enumerate(copies)]
    loads[0].start()
    around = [dev(dy=1), dev(dy=-1), dev(dz=1), dev(dz=-1)]
    partners = [dev(dc=1), dev(dx=2)] + [dev(dx=dx, dc=dc) for dx in (1, 3) for dc in (0, 1)] + around
    barrier = pltpu.get_barrier_semaphore()
    for partner in partners:
        pl.semaphore_signal(barrier, inc=1, device_id=partner, device_id_type=MESH)
    for load in loads[1:]:
        load.start()
    loads[0].wait()
    points = panel_t[...].T
    panel[0] = points
    for p in range(8):
        for h in (0, 1):
            panel[3, 128 * h + 16 * p : 128 * h + 16 * p + 16] = points[32 * p + 16 * h : 32 * p + 16 * h + 16]

    for load in loads[1:6]:
        load.wait()
    live = jnp.sum(counts_ref[...], axis=1, keepdims=True)
    keep = lax.broadcasted_iota(jnp.int32, (1, SLOTS), 1) < live
    slot_atom = jnp.where(keep, fatom_ref[...], -1)
    atoms = lax.broadcasted_iota(jnp.int32, (ATOMS, SLOTS), 0)
    hot[...] = jnp.where(atoms == slot_atom, 1.0, 0.0).astype(BF16)
    cells = lax.broadcasted_iota(jnp.int32, (CELLS, ATOMS), 0)
    member[...] = jnp.where(cells == cell_ref[...], 1.0, 0.0).astype(BF16)
    ftarget = ftarget_ref[...].astype(F32)
    ftarget = jnp.concatenate([ftarget[k : k + 1] for k in range(8)], axis=1)
    target[:, :SLOTS] = jnp.broadcast_to(jnp.where(keep, ftarget, 0.0), (16, SLOTS)).astype(BF16)
    target[:, SLOTS:] = jnp.broadcast_to(etarget_ref[...].astype(F32), (16, CELLS)).astype(BF16)
    members = dot(jnp.ones((16, ATOMS), BF16), member[...], NT)[0:1]
    members = jnp.maximum(members, 1.0)
    def make_rows(j, first, count):
        at, own = (0, c) if j == 0 else (1, j - 1)
        rows = slice(first, first + count)
        points = panel[j, rows]
        products = dot(points, desc[...], NN)
        high, low = halves(products)
        atom_dots = dot(high, hot[...], NN) + dot(low, hot[...], NN)
        grad_dots = dot(points, grad[...], NN)
        kern[at, own, rows, :SLOTS] = (atom_dots * atom_dots * atom_dots * grad_dots).astype(BF16)
        squares = products * products
        high, low = halves(squares * squares)
        energy = dot(high, member[...], NT) + dot(low, member[...], NT)
        kern[at, own, rows, SLOTS:] = (energy / members).astype(BF16)

    def send(src, dst, send_sem, recv_sem, to):
        remote(src, dst, send_sem, recv_sem, to).start()

    quarter = ((1 + c) * y + (2 - c) * z) % 4 * 32

    def share(h):
        return pl.ds(pl.multiple_of(128 * h + quarter, 32), 32)

    def fetch(j, h):
        src = panel.at[0 if j == 1 else 3, share(h)]
        send(src, panel.at[j, share(h)], x_send, x_recv.at[j - 1, h], dev(dx=-j))

    def fetch_c(now):
        @pl.when(now)
        def _():
            fetch(2, 0)
            fetch(2, 1)

    def forward(j, h):
        block = panel.at[j, share(h)]
        arrived(block, x_recv.at[j - 1, h])
        side = 1 - 2 * h
        targets = (dev(dy=1 - c, dz=c), dev(dy=c - 1, dz=-c), dev(dy=c * side, dz=(1 - c) * side))
        for to in targets:
            send(block, block, f_send, f_recv.at[j - 1, h], to)

    def gathered(j, h):
        arrived(panel.at[j, pl.ds(128 * h, 96)], f_recv.at[j - 1, h])

    line = (1 - c) * z + c * y

    far_first = (4, 3, 5, 2, 6, 1, 7)

    def tell(n):
        for to in around:
            pl.semaphore_signal(token.at[n], inc=1, device_id=to, device_id_type=MESH)

    def hear(n):
        pl.semaphore_wait(token.at[n], len(around))

    def multiply_a():
        blocks = [dot(kern[0, c], kern[0, a], NT).astype(BF16) for a in (0, 1)]
        for core, pieces in enumerate((((0, 0), (0, 1), (0, 2), (1, 1), (1, 3)), ((0, 2), (0, 3), (0, 1), (1, 3), (1, 0)))):

            @pl.when(c == core)
            def _(pieces=pieces):
                for n, (h, w) in enumerate(pieces):
                    at = 128 * (w % 2)
                    part1[0, n] = blocks[w // 2][128 * h : 128 * h + 128, at : at + 128]

    def step1_a(now):
        for n in range(5):
            to = n + 3 * c
            k = (to - z + 8) % 8
            here = k == 0
            slot = jnp.where(here, 0, k - 1)
            copy = remote(part1.at[0, n], recv1.at[0, slot], s1_send.at[0], s1_recv.at[0], dev(dz=to - z + 8))

            @pl.when(jnp.logical_not(here) & now)
            def _(copy=copy):
                copy.start()

    def multiply_b():
        for a in (0, 1):
            block = dot(kern[1, 0], kern[0, a], NT).astype(BF16)
            for h in (0, 1):
                for w in (0, 1):
                    part1[1, 4 * w + 2 * h + a] = block[128 * h : 128 * h + 128, 128 * w : 128 * w + 128]

    def multiply_half(h):
        rows = kern[1, 1, 128 * h : 128 * h + 128]
        for a in (0, 1):
            block = dot(rows, kern[0, a], NT).astype(BF16)
            for w in (0, 1):
                at = 64 * h + 16 * (2 * a + w)
                for p in range(8):
                    part1[2, p, at : at + 16] = block[16 * p : 16 * p + 16, 128 * w : 128 * w + 128]

    def step1_b(now):
        @pl.when(now)
        def _():
            for k in far_first:
                to = dev(dz=(1 - c) * k, dy=c * k)
                send(part1.at[1, (line + k) % 8], recv1.at[1, k - 1], s1_send.at[1], s1_recv.at[1], to)

    def step1_half(h):
        rows = pl.ds(64 * h, 64)
        for k in far_first:
            src = part1.at[2, (y + k) % 8, rows]
            send(src, recv1.at[2, k - 1, rows], s1_send.at[2], s1_recv.at[2 + h], dev(dy=k))

    pl.semaphore_wait(barrier, len(partners))
    fetch(1, 0)
    fetch(1, 1)
    tell(0)
    for load in loads[6:]:
        load.wait()
    make_rows(0, 0, 256)
    send(kern.at[0, c], kern.at[0, c], d_send, d_recv, dev(dc=1))
    hear(0)
    tell(1)
    part = dot(target[...], kern[0, c], NT)[0:8]
    rpart[...] = part
    forward(1, 0)
    fetch_c(x == 0)
    hear(1)
    tell(2)
    forward(1, 1)
    fetch_c(x != 0)
    arrived(kern.at[0, 1 - c], d_recv)
    multiply_a()
    hear(2)
    for k in far_first:
        send(rpart, rz.at[k - 1], rz_send, rz_recv, dev(dz=k))
    forward(2, 0)
    gathered(1, 0)
    make_rows(1, 0, 128)
    forward(2, 1)
    step1_a(x < 2)
    gathered(1, 1)
    make_rows(1, 128, 128)
    multiply_b()
    step1_b(x != 2)

    gathered(2, 0)
    make_rows(2, 0, 128)
    multiply_half(0)
    step1_half(0)
    step1_a(x == 3)

    arrived(rz, rz_recv)
    for to in (dev(dc=1), dev(dx=-1), dev(dx=-1, dc=1)):
        pl.semaphore_signal(token.at[3], inc=1, device_id=to, device_id_type=MESH)
    total = jnp.zeros((8, PTS), F32)
    for s in range(8):
        slot = (z - s + 7) % 8
        value = rz[jnp.minimum(slot, 6)]
        total = total + jnp.where(slot == 7, part, value)
    rsum[...] = total
    for k in far_first:
        send(rsum, ry.at[k - 1], ry_send, ry_recv, dev(dy=k))

    gathered(2, 1)
    make_rows(2, 128, 128)
    multiply_half(1)
    step1_half(1)
    step1_b(x == 2)
    step1_a(x == 2)

    pl.semaphore_wait(token.at[3], 3)

    def deliver(n, src, dst, to):
        here = (to[0] == r) & (to[1] == b)

        @pl.when(here)
        def _():
            pltpu.make_async_copy(src, dst, s2_recv).start()

        @pl.when(jnp.logical_not(here))
        def _():
            send(src, dst, s2_send.at[n], s2_recv, to)

    def first_sum(j, mine, rows, sem):
        arrived(recv1.at[j, :, rows], sem)
        acc = part1[j, mine, rows].astype(F32)
        for k in range(7):
            acc = acc + recv1[j, k, rows].astype(F32)
        return acc

    n = z - 3 * c
    down = 2 * c + jnp.where(n >= 3, 1, 0)
    first = jnp.where(n == 3, 1, jnp.where(n == 4, 3, n))
    second = jnp.where(n == 0, 2, jnp.where(n == 2, 1, jnp.where(n == 4, 0, 3)))
    across = jnp.where(c == 0, first, second)

    holds = (n >= 0) & (n < 5)
    targets_a = [((2 * x + down // 2) * 8 + 4 * (down % 2) + k, 2 * x + across // 2) for k in range(4)]
    targets_t = [((2 * x + across // 2) * 8 + 4 * (across % 2) + k, 2 * x + down // 2) for k in range(4)]

    def step2_a(now):
        @pl.when(holds & now)
        def _():
            acc = first_sum(0, n, pl.ds(0, 128), s1_recv.at[0])
            part2[0] = acc.astype(BF16)
            for k in range(4):
                src = part2.at[0, pl.ds(32 * k, 32)]
                deliver(0, src, recv2.at[across % 2, y], targets_a[k])

            @pl.when(down != across)
            def _():
                part2[4] = acc.T.astype(BF16)
                for k in range(4):
                    src = part2.at[4, pl.ds(32 * k, 32)]
                    deliver(1, src, recv2.at[down % 2, y], targets_t[k])

    w, h, a = line // 4, (line // 2) % 2, line % 2
    cross, block = z + y - line, 2 * ((x + 1) % 4) + c

    def step2_b(now):
        @pl.when(now)
        def _():
            acc = first_sum(1, line, pl.ds(0, 128), s1_recv.at[1])
            part2[1] = acc.astype(BF16)
            part2[3] = acc.T.astype(BF16)
            for k in range(4):
                src = part2.at[3, pl.ds(32 * k, 32)]
                send(src, recv2.at[h, cross], s2_send.at[2], s2_recv, ((2 * x + a) * 8 + 4 * w + k, block))
            for k in range(4):
                src = part2.at[1, pl.ds(32 * k, 32)]
                deliver(3, src, recv2.at[w, cross], (block * 8 + 4 * h + k, 2 * x + a))

    def step2_c():
        for half in (0, 1):
            rows = pl.ds(64 * half, 64)
            part2[2, rows] = first_sum(2, y, rows, s1_recv.at[2 + half]).astype(BF16)
            for n in range(4):
                src = part2.at[2, pl.ds(64 * half + 16 * n, 16)]
                dst = recv2.at[n % 2, z, pl.ds(16 * half, 16)]
                to = ((2 * ((x + 2) % 4) + c) * 8 + y, 2 * x + n // 2)
                deliver(4, src, dst, to)

    step2_a(x < 2)
    step2_b(x != 2)
    step2_c()
    step2_b(x == 2)
    step2_a(x >= 2)

    arrived(ry, ry_recv)
    final = jnp.zeros((8, PTS), F32)
    for s in range(8):
        slot = (y - s + 7) % 8
        value = ry[jnp.minimum(slot, 6)]
        final = final + jnp.where(slot == 7, total, value)
    right_ref[...] = final[0:1] / ROWS_ALL

    arrived(panel.at[0, pl.ds(0, 128)], x_send)
    arrived(panel.at[pl.ds(0, 3), pl.ds(0, 128)], f_send)
    arrived(kern.at[0, c], d_send)
    arrived(rz, rz_send)
    arrived(ry, ry_send)
    arrived(recv1.at[1], s1_send.at[1])
    arrived(recv1.at[2], s1_send.at[2])
    arrived(part2.at[2], s2_send.at[2])

    def left(ref, few, many, fewer, sem, active=True):
        @pl.when(active & fewer)
        def _():
            arrived(ref.at[pl.ds(0, few)], sem)

        @pl.when(active & jnp.logical_not(fewer))
        def _():
            arrived(ref.at[pl.ds(0, many)], sem)

    def among(targets):
        found = False
        for to in targets:
            found = found | ((to[0] == r) & (to[1] == b))
        return found

    flat = part2.at[0]
    left(recv1.at[0], 4, 5, holds, s1_send.at[0])
    left(flat, 96, 128, among(targets_a), s2_send.at[0], holds)
    left(flat, 96, 128, among(targets_t), s2_send.at[1], holds & (down != across))
    left(flat, 96, 128, among([(block * 8 + 4 * h + k, 2 * x + a) for k in range(4)]), s2_send.at[3])
    left(flat, 64, 128, z == 2 * ((x + 2) % 4) + c, s2_send.at[4])

    arrived(recv2, s2_recv)
    for w2 in (0, 1):
        acc = recv2[w2, 0].astype(F32)
        for s in range(1, 8):
            acc = acc + recv2[w2, s].astype(F32)
        gram_ref[:, 128 * w2 : 128 * w2 + 128] = acc / ROWS_ALL


def body(atom_desc, sparse_panel, atom_cell, energy_target, force_counts, force_atom, force_grad, force_target):
    vmem, hbm = pl.BlockSpec(memory_space=pltpu.VMEM), pl.BlockSpec(memory_space=pltpu.HBM)
    dma, sem = pltpu.VMEM, pltpu.SemaphoreType.DMA
    operands = (
        atom_desc,
        sparse_panel.T,
        atom_cell.reshape(1, ATOMS),
        energy_target.reshape(1, CELLS),
        force_counts.reshape(1, CELLS),
        force_atom.reshape(1, SLOTS),
        force_grad,
        force_target.reshape(8, 128),
    )
    gram, right = pl.pallas_call(
        kernel,
        out_shape=(jax.ShapeDtypeStruct((32, PTS), F32), jax.ShapeDtypeStruct((1, PTS), F32)),
        in_specs=[hbm] * 8,
        out_specs=(vmem, vmem),
        scratch_shapes=[
            dma((D, ATOMS), BF16),
            dma((D, PTS), BF16),
            dma((1, ATOMS), jnp.int32),
            dma((1, CELLS), BF16),
            dma((1, CELLS), jnp.int32),
            dma((1, SLOTS), jnp.int32),
            dma((D, SLOTS), BF16),
            dma((8, 128), BF16),
            dma((4, PTS, D), BF16),
            dma((ATOMS, SLOTS), BF16),
            dma((CELLS, ATOMS), BF16),
            dma((2, 2, PTS, COLS), BF16),
            dma((16, COLS), BF16),
            dma((3, 8, 128, 128), BF16),
            dma((3, 7, 128, 128), BF16),
            dma((5, 128, 128), BF16),
            dma((2, 8, 32, 128), BF16),
            dma((8, PTS), F32),
            dma((7, 8, PTS), F32),
            dma((8, PTS), F32),
            dma((7, 8, PTS), F32),
            sem((8,)),
            sem,
            sem((2, 2)),
            sem,
            sem((2, 2)),
            sem,
            sem,
            sem((3,)),
            sem((4,)),
            sem((5,)),
            sem,
            sem,
            sem,
            sem,
            sem,
            pltpu.SemaphoreType.REGULAR((4,)),
        ],
        compiler_params=pltpu.CompilerParams(
            collective_id=0, has_side_effects=True, vmem_limit_bytes=24 * 2**20
        ),
        name="gram",
    )(*[pltpu.with_memory_space_constraint(operand, pltpu.HBM) for operand in operands])
    return gram, right.reshape(PTS)


def solution(mesh):
    in_specs = (
        P(None, "rows"),
        P("blk", None),
        P("rows"),
        P("rows"),
        P("rows"),
        P("rows"),
        P(None, "rows"),
        P("rows"),
    )
    out_specs = (P("rows", "blk"), P("blk"))
    return jax.shard_map(body, mesh=mesh, in_specs=in_specs, out_specs=out_specs, check_vma=False)
```

```python
import jax
import jax.numpy as jnp
from jax import lax
from jax.experimental import pallas as pl
from jax.experimental.pallas import tpu as pltpu
from jax.sharding import PartitionSpec as P

MESH = pl.DeviceIdType.MESH
F32, BF16 = jnp.float32, jnp.bfloat16
D, PTS, ATOMS, CELLS, SLOTS = 1000, 256, 512, 32, 1024
COLS = SLOTS + CELLS
ROWS_ALL = 34816.0
NN = (((1,), (0,)), ((), ()))
NT = (((1,), (1,)), ((), ()))


def dot(a, b, dims):
    return lax.dot_general(a, b, dims, preferred_element_type=F32)


def halves(value):
    high = value.astype(BF16)
    return high, (value - high.astype(F32)).astype(BF16)


def kernel(
    desc_hbm, panel_hbm, cell_hbm, etarget_hbm, counts_hbm, fatom_hbm, grad_hbm, ftarget_hbm,
    gram_ref, right_ref,
    desc, panel_t, cell_ref, etarget_ref, counts_ref, fatom_ref, grad, ftarget_ref,
    panel, hot, member, kern, target, part1, recv1, part2, recv2,
    rpart, rz, rsum, ry,
    load_sem, x_send, x_recv, f_send, f_recv, d_send, d_recv, s1_send, s1_recv, s2_send, s2_recv,
    rz_send, rz_recv, ry_send, ry_recv, token,
):
    r, b = lax.axis_index("rows"), lax.axis_index("blk")
    z, y, x, c = r // 8, r % 8, b // 2, b % 2

    def dev(dz=0, dy=0, dx=0, dc=0):
        return ((z + dz) % 8) * 8 + (y + dy) % 8, ((x + dx) % 4) * 2 + (c + dc) % 2

    def remote(src, dst, send, recv, to):
        return pltpu.make_async_remote_copy(
            src_ref=src, dst_ref=dst, send_sem=send, recv_sem=recv, device_id=to, device_id_type=MESH
        )

    def arrived(ref, sem):
        pltpu.make_async_copy(ref, ref, sem).wait()

    copies = (
        (panel_hbm, panel_t), (fatom_hbm, fatom_ref), (counts_hbm, counts_ref), (cell_hbm, cell_ref),
        (etarget_hbm, etarget_ref), (ftarget_hbm, ftarget_ref), (desc_hbm, desc), (grad_hbm, grad),
    )
    loads = [pltpu.make_async_copy(src, dst, load_sem.at[n]) for n, (src, dst) in enumerate(copies)]
    around = [dev(dy=1), dev(dy=-1), dev(dz=1), dev(dz=-1)]
    partners = [dev(dc=1), dev(dx=2)] + [dev(dx=dx, dc=dc) for dx in (1, 3) for dc in (0, 1)] + around
    barrier = pltpu.get_barrier_semaphore()
    for partner in partners:
        pl.semaphore_signal(barrier, inc=1, device_id=partner, device_id_type=MESH)
    for load in loads:
        load.start()
    loads[0].wait()
    points = panel_t[...].T
    panel[0] = points
    for p in range(8):
        for h in (0, 1):
            panel[3, 128 * h + 16 * p : 128 * h + 16 * p + 16] = points[32 * p + 16 * h : 32 * p + 16 * h + 16]

    for load in loads[1:6]:
        load.wait()
    live = jnp.sum(counts_ref[...], axis=1, keepdims=True)
    keep = lax.broadcasted_iota(jnp.int32, (1, SLOTS), 1) < live
    slot_atom = jnp.where(keep, fatom_ref[...], -1)
    atoms = lax.broadcasted_iota(jnp.int32, (ATOMS, SLOTS), 0)
    hot[...] = jnp.where(atoms == slot_atom, 1.0, 0.0).astype(BF16)
    cells = lax.broadcasted_iota(jnp.int32, (CELLS, ATOMS), 0)
    member[...] = jnp.where(cells == cell_ref[...], 1.0, 0.0).astype(BF16)
    ftarget = ftarget_ref[...].astype(F32)
    ftarget = jnp.concatenate([ftarget[k : k + 1] for k in range(8)], axis=1)
    target[:, :SLOTS] = jnp.broadcast_to(jnp.where(keep, ftarget, 0.0), (16, SLOTS)).astype(BF16)
    target[:, SLOTS:] = jnp.broadcast_to(etarget_ref[...].astype(F32), (16, CELLS)).astype(BF16)
    members = dot(jnp.ones((16, ATOMS), BF16), member[...], NT)[0:1]
    members = jnp.maximum(members, 1.0)
    def make_rows(j, first, count):
        at, own = (0, c) if j == 0 else (1, j - 1)
        rows = slice(first, first + count)
        points = panel[j, rows]
        products = dot(points, desc[...], NN)
        high, low = halves(products)
        atom_dots = dot(high, hot[...], NN) + dot(low, hot[...], NN)
        grad_dots = dot(points, grad[...], NN)
        kern[at, own, rows, :SLOTS] = (atom_dots * atom_dots * atom_dots * grad_dots).astype(BF16)
        squares = products * products
        high, low = halves(squares * squares)
        energy = dot(high, member[...], NT) + dot(low, member[...], NT)
        kern[at, own, rows, SLOTS:] = (energy / members).astype(BF16)

    def send(src, dst, send_sem, recv_sem, to):
        remote(src, dst, send_sem, recv_sem, to).start()

    quarter = ((1 + c) * y + (2 - c) * z) % 4 * 32

    def share(h):
        return pl.ds(pl.multiple_of(128 * h + quarter, 32), 32)

    def fetch(j, h):
        src = panel.at[0 if j == 1 else 3, share(h)]
        send(src, panel.at[j, share(h)], x_send, x_recv.at[j - 1, h], dev(dx=-j))

    def fetch_c(now):
        @pl.when(now)
        def _():
            fetch(2, 0)
            fetch(2, 1)

    def forward(j, h):
        block = panel.at[j, share(h)]
        arrived(block, x_recv.at[j - 1, h])
        side = 1 - 2 * h
        targets = (dev(dy=1 - c, dz=c), dev(dy=c - 1, dz=-c), dev(dy=c * side, dz=(1 - c) * side))
        for to in targets:
            send(block, block, f_send, f_recv.at[j - 1, h], to)

    def gathered(j, h):
        arrived(panel.at[j, pl.ds(128 * h, 96)], f_recv.at[j - 1, h])

    line = (1 - c) * z + c * y

    far_first = (4, 3, 5, 2, 6, 1, 7)

    def tell(n):
        for to in around:
            pl.semaphore_signal(token.at[n], inc=1, device_id=to, device_id_type=MESH)

    def hear(n):
        pl.semaphore_wait(token.at[n], len(around))

    def multiply_a():
        blocks = [dot(kern[0, c], kern[0, a], NT).astype(BF16) for a in (0, 1)]
        for core, pieces in enumerate((((0, 0), (0, 1), (0, 2), (1, 1), (1, 3)), ((0, 2), (0, 3), (0, 1), (1, 3), (1, 0)))):

            @pl.when(c == core)
            def _(pieces=pieces):
                for n, (h, w) in enumerate(pieces):
                    at = 128 * (w % 2)
                    part1[0, n] = blocks[w // 2][128 * h : 128 * h + 128, at : at + 128]

    def step1_a(now):
        for n in range(5):
            to = n + 3 * c
            k = (to - z + 8) % 8
            here = k == 0
            slot = jnp.where(here, 0, k - 1)
            copy = remote(part1.at[0, n], recv1.at[0, slot], s1_send.at[0], s1_recv.at[0], dev(dz=to - z + 8))

            @pl.when(jnp.logical_not(here) & now)
            def _(copy=copy):
                copy.start()

    def multiply_b():
        for a in (0, 1):
            block = dot(kern[1, 0], kern[0, a], NT).astype(BF16)
            for h in (0, 1):
                for w in (0, 1):
                    part1[1, 4 * w + 2 * h + a] = block[128 * h : 128 * h + 128, 128 * w : 128 * w + 128]

    def multiply_half(h):
        rows = kern[1, 1, 128 * h : 128 * h + 128]
        for a in (0, 1):
            block = dot(rows, kern[0, a], NT).astype(BF16)
            for w in (0, 1):
                at = 64 * h + 16 * (2 * a + w)
                for p in range(8):
                    part1[2, p, at : at + 16] = block[16 * p : 16 * p + 16, 128 * w : 128 * w + 128]

    def step1_b(now):
        @pl.when(now)
        def _():
            for k in far_first:
                to = dev(dz=(1 - c) * k, dy=c * k)
                send(part1.at[1, (line + k) % 8], recv1.at[1, k - 1], s1_send.at[1], s1_recv.at[1], to)

    def step1_half(h):
        rows = pl.ds(64 * h, 64)
        for k in far_first:
            src = part1.at[2, (y + k) % 8, rows]
            send(src, recv1.at[2, k - 1, rows], s1_send.at[2], s1_recv.at[2 + h], dev(dy=k))

    pl.semaphore_wait(barrier, len(partners))
    fetch(1, 0)
    fetch(1, 1)
    tell(0)
    for load in loads[6:]:
        load.wait()
    make_rows(0, 0, 256)
    send(kern.at[0, c], kern.at[0, c], d_send, d_recv, dev(dc=1))
    hear(0)
    tell(1)
    part = dot(target[...], kern[0, c], NT)[0:8]
    rpart[...] = part
    forward(1, 0)
    fetch_c(x == 0)
    hear(1)
    tell(2)
    forward(1, 1)
    fetch_c(x != 0)
    arrived(kern.at[0, 1 - c], d_recv)
    multiply_a()
    hear(2)
    for k in far_first:
        send(rpart, rz.at[k - 1], rz_send, rz_recv, dev(dz=k))
    forward(2, 0)
    gathered(1, 0)
    make_rows(1, 0, 128)
    forward(2, 1)
    step1_a(x < 2)
    gathered(1, 1)
    make_rows(1, 128, 128)
    multiply_b()
    step1_b(x != 2)

    gathered(2, 0)
    make_rows(2, 0, 128)
    multiply_half(0)
    step1_half(0)

    arrived(rz, rz_recv)
    for to in (dev(dc=1), dev(dx=-1), dev(dx=-1, dc=1)):
        pl.semaphore_signal(token.at[3], inc=1, device_id=to, device_id_type=MESH)
    total = jnp.zeros((8, PTS), F32)
    for s in range(8):
        slot = (z - s + 7) % 8
        value = rz[jnp.minimum(slot, 6)]
        total = total + jnp.where(slot == 7, part, value)
    rsum[...] = total
    for k in far_first:
        send(rsum, ry.at[k - 1], ry_send, ry_recv, dev(dy=k))

    gathered(2, 1)
    make_rows(2, 128, 128)
    multiply_half(1)
    step1_half(1)
    step1_b(x == 2)
    step1_a(x >= 2)

    pl.semaphore_wait(token.at[3], 3)

    def deliver(n, src, dst, to):
        here = (to[0] == r) & (to[1] == b)

        @pl.when(here)
        def _():
            pltpu.make_async_copy(src, dst, s2_recv).start()

        @pl.when(jnp.logical_not(here))
        def _():
            send(src, dst, s2_send.at[n], s2_recv, to)

    def first_sum(j, mine, rows, sem):
        arrived(recv1.at[j, :, rows], sem)
        acc = part1[j, mine, rows].astype(F32)
        for k in range(7):
            acc = acc + recv1[j, k, rows].astype(F32)
        return acc

    n = z - 3 * c
    down = 2 * c + jnp.where(n >= 3, 1, 0)
    first = jnp.where(n == 3, 1, jnp.where(n == 4, 3, n))
    second = jnp.where(n == 0, 2, jnp.where(n == 2, 1, jnp.where(n == 4, 0, 3)))
    across = jnp.where(c == 0, first, second)

    holds = (n >= 0) & (n < 5)
    targets_a = [((2 * x + down // 2) * 8 + 4 * (down % 2) + k, 2 * x + across // 2) for k in range(4)]
    targets_t = [((2 * x + across // 2) * 8 + 4 * (across % 2) + k, 2 * x + down // 2) for k in range(4)]

    def step2_a(now):
        @pl.when(holds & now)
        def _():
            acc = first_sum(0, n, pl.ds(0, 128), s1_recv.at[0])
            part2[0] = acc.astype(BF16)
            for k in range(4):
                src = part2.at[0, pl.ds(32 * k, 32)]
                deliver(0, src, recv2.at[across % 2, y], targets_a[k])

            @pl.when(down != across)
            def _():
                part2[4] = acc.T.astype(BF16)
                for k in range(4):
                    src = part2.at[4, pl.ds(32 * k, 32)]
                    deliver(1, src, recv2.at[down % 2, y], targets_t[k])

    w, h, a = line // 4, (line // 2) % 2, line % 2
    cross, block = z + y - line, 2 * ((x + 1) % 4) + c

    def step2_b(now):
        @pl.when(now)
        def _():
            acc = first_sum(1, line, pl.ds(0, 128), s1_recv.at[1])
            part2[1] = acc.astype(BF16)
            part2[3] = acc.T.astype(BF16)
            for k in range(4):
                src = part2.at[3, pl.ds(32 * k, 32)]
                send(src, recv2.at[h, cross], s2_send.at[2], s2_recv, ((2 * x + a) * 8 + 4 * w + k, block))
            for k in range(4):
                src = part2.at[1, pl.ds(32 * k, 32)]
                deliver(3, src, recv2.at[w, cross], (block * 8 + 4 * h + k, 2 * x + a))

    def step2_c():
        for half in (0, 1):
            rows = pl.ds(64 * half, 64)
            part2[2, rows] = first_sum(2, y, rows, s1_recv.at[2 + half]).astype(BF16)
            for n in range(4):
                src = part2.at[2, pl.ds(64 * half + 16 * n, 16)]
                dst = recv2.at[n % 2, z, pl.ds(16 * half, 16)]
                to = ((2 * ((x + 2) % 4) + c) * 8 + y, 2 * x + n // 2)
                deliver(4, src, dst, to)

    step2_a(x < 2)
    step2_b(x != 2)
    step2_c()
    step2_b(x == 2)
    step2_a(x >= 2)

    arrived(ry, ry_recv)
    final = jnp.zeros((8, PTS), F32)
    for s in range(8):
        slot = (y - s + 7) % 8
        value = ry[jnp.minimum(slot, 6)]
        final = final + jnp.where(slot == 7, total, value)
    right_ref[...] = final[0:1] / ROWS_ALL

    arrived(panel.at[0, pl.ds(0, 128)], x_send)
    arrived(panel.at[pl.ds(0, 3), pl.ds(0, 128)], f_send)
    arrived(kern.at[0, c], d_send)
    arrived(rz, rz_send)
    arrived(ry, ry_send)
    arrived(recv1.at[1], s1_send.at[1])
    arrived(recv1.at[2], s1_send.at[2])
    arrived(part2.at[2], s2_send.at[2])

    def left(ref, few, many, fewer, sem, active=True):
        @pl.when(active & fewer)
        def _():
            arrived(ref.at[pl.ds(0, few)], sem)

        @pl.when(active & jnp.logical_not(fewer))
        def _():
            arrived(ref.at[pl.ds(0, many)], sem)

    def among(targets):
        found = False
        for to in targets:
            found = found | ((to[0] == r) & (to[1] == b))
        return found

    flat = part2.at[0]
    left(recv1.at[0], 4, 5, holds, s1_send.at[0])
    left(flat, 96, 128, among(targets_a), s2_send.at[0], holds)
    left(flat, 96, 128, among(targets_t), s2_send.at[1], holds & (down != across))
    left(flat, 96, 128, among([(block * 8 + 4 * h + k, 2 * x + a) for k in range(4)]), s2_send.at[3])
    left(flat, 64, 128, z == 2 * ((x + 2) % 4) + c, s2_send.at[4])

    arrived(recv2, s2_recv)
    for w2 in (0, 1):
        acc = recv2[w2, 0].astype(F32)
        for s in range(1, 8):
            acc = acc + recv2[w2, s].astype(F32)
        gram_ref[:, 128 * w2 : 128 * w2 + 128] = acc / ROWS_ALL


def body(atom_desc, sparse_panel, atom_cell, energy_target, force_counts, force_atom, force_grad, force_target):
    vmem, hbm = pl.BlockSpec(memory_space=pltpu.VMEM), pl.BlockSpec(memory_space=pltpu.HBM)
    dma, sem = pltpu.VMEM, pltpu.SemaphoreType.DMA
    operands = (
        atom_desc,
        sparse_panel.T,
        atom_cell.reshape(1, ATOMS),
        energy_target.reshape(1, CELLS),
        force_counts.reshape(1, CELLS),
        force_atom.reshape(1, SLOTS),
        force_grad,
        force_target.reshape(8, 128),
    )
    gram, right = pl.pallas_call(
        kernel,
        out_shape=(jax.ShapeDtypeStruct((32, PTS), F32), jax.ShapeDtypeStruct((1, PTS), F32)),
        in_specs=[hbm] * 8,
        out_specs=(vmem, vmem),
        scratch_shapes=[
            dma((D, ATOMS), BF16),
            dma((D, PTS), BF16),
            dma((1, ATOMS), jnp.int32),
            dma((1, CELLS), BF16),
            dma((1, CELLS), jnp.int32),
            dma((1, SLOTS), jnp.int32),
            dma((D, SLOTS), BF16),
            dma((8, 128), BF16),
            dma((4, PTS, D), BF16),
            dma((ATOMS, SLOTS), BF16),
            dma((CELLS, ATOMS), BF16),
            dma((2, 2, PTS, COLS), BF16),
            dma((16, COLS), BF16),
            dma((3, 8, 128, 128), BF16),
            dma((3, 7, 128, 128), BF16),
            dma((5, 128, 128), BF16),
            dma((2, 8, 32, 128), BF16),
            dma((8, PTS), F32),
            dma((7, 8, PTS), F32),
            dma((8, PTS), F32),
            dma((7, 8, PTS), F32),
            sem((8,)),
            sem,
            sem((2, 2)),
            sem,
            sem((2, 2)),
            sem,
            sem,
            sem((3,)),
            sem((4,)),
            sem((5,)),
            sem,
            sem,
            sem,
            sem,
            sem,
            pltpu.SemaphoreType.REGULAR((4,)),
        ],
        compiler_params=pltpu.CompilerParams(
            collective_id=0, has_side_effects=True, vmem_limit_bytes=24 * 2**20
        ),
        name="gram",
    )(*[pltpu.with_memory_space_constraint(operand, pltpu.HBM) for operand in operands])
    return gram, right.reshape(PTS)


def solution(mesh):
    in_specs = (
        P(None, "rows"),
        P("blk", None),
        P("rows"),
        P("rows"),
        P("rows"),
        P("rows"),
        P(None, "rows"),
        P("rows"),
    )
    out_specs = (P("rows", "blk"), P("blk"))
    return jax.shard_map(body, mesh=mesh, in_specs=in_specs, out_specs=out_specs, check_vma=False)
```
